256 devices in a mesh: dp: 64 (over z, x, core), tensor: 4 (over y).
Axes of the slice: x: 4, y: 4, z: 8, core: 2. Of those that a mesh axis runs over, the one named last changes fastest.
Arguments:
- queries: bfloat16 [8192, 5120], P('dp', 'tensor'), may hold values from -200 to 200
- keys: bfloat16 [8192, 1024], P('dp', 'tensor'), may hold values from -8 to 8
- values: bfloat16 [8192, 1024], P('dp', 'tensor'), may hold values from -6 to 6
- output_gradient: bfloat16 [8192, 5120], P('dp', 'tensor'), may hold values from -6 to 6
- prompt_slot_keys: bfloat16 [2048, 1024], P('dp', 'tensor'), may hold values from -6 to 6
- prompt_slot_values: bfloat16 [2048, 1024], P('dp', 'tensor'), may hold values from -6 to 6
- query_weight: bfloat16 [5120, 5120], P('dp', 'tensor'), may hold values from -0.078125 to 0.078125
- lengths: int32 [128], replicated, may hold values from 1 to 128, 8192 in all
- prompt_owner: int32 [8], replicated, may hold values from 0 to 7, each once
Outputs:
- grad_queries: bfloat16 [8192, 5120], P('dp', 'tensor')
- grad_keys: bfloat16 [8192, 1024], P('dp', 'tensor')
- grad_values: bfloat16 [8192, 1024], P('dp', 'tensor')
- grad_prompt_keys: bfloat16 [2048, 1024], P('dp', 'tensor')
- grad_prompt_values: bfloat16 [2048, 1024], P('dp', 'tensor')
- grad_input: bfloat16 [8192, 5120], P('dp', 'tensor')
The draws below stay inside these ranges and needn't reach their ends.
Inputs may be any that keep to these rules, and one draw needn't show every extreme that they name: `lengths`: lengths of the 128 responses in packing order; response r answers prompt r // 16; they sum to 8192 and the largest is exactly 128. A permutation: prompt p sits in slot prompt_owner[p], the rows p' * 256 to (p' + 1) * 256 - 1 of the prompt arrays with p' = prompt_owner[p].
All inputs are finite; a program needn't handle non-finite values.
Results may differ from the reference program's by a relative error of at most 0.015.
Values may be sent and summed in bfloat16 or wider, within the bound.
A program may use at most 64 MiB of HBM per device.

```python
import math
import jax
import jax.numpy as jnp
import numpy as np
from jax import lax

D = 5120
QUERY_HEADS = 40
KEY_VALUE_HEADS = 8
HEAD_SIZE = 128
IMAGE_PROMPTS = 8
RESP_PER = 16
TOKENS_PER_SHARD = 128
RESPONSES = 128
PACKED_TOKENS = 8192
PROMPT_LENGTH = 256


def shared_keys(key):
    base_offset = jax.random.normal(key, (PACKED_TOKENS, KEY_VALUE_HEADS * HEAD_SIZE), jnp.float32)
    rows = jnp.arange(PACKED_TOKENS)
    picked = (rows % 61 == 1)[:, None]
    return (jnp.where(picked, base_offset, base_offset), picked)


def draw_keys(key, part):
    current_keys, picked = shared_keys(key)
    return current_keys.astype(jnp.bfloat16)


def draw_queries(key, part):
    strength = 0.0
    current_keys, picked = shared_keys(key)
    key = jax.random.fold_in(key, 3)
    own = jax.random.normal(key, (PACKED_TOKENS, QUERY_HEADS * HEAD_SIZE), jnp.float32)
    rows = jnp.arange(PACKED_TOKENS)
    scale_factor = (10.0 + 4.0 * (rows // 61 % 4)).astype(jnp.float32)[:, None, None, None]
    aligned_rows = scale_factor * jnp.broadcast_to(current_keys.reshape(PACKED_TOKENS, KEY_VALUE_HEADS, 1, HEAD_SIZE), (PACKED_TOKENS, KEY_VALUE_HEADS, QUERY_HEADS // KEY_VALUE_HEADS, HEAD_SIZE))
    aligned_rows = aligned_rows.reshape(PACKED_TOKENS, QUERY_HEADS * HEAD_SIZE)
    return jnp.where(picked & (strength > 0.5), aligned_rows, own).astype(jnp.bfloat16)


def level_of(stream_key, shape, split, smallest, high):
    gain, own = 1.0, jax.random.fold_in(stream_key, 6)
    for dim, blocks in split:
        heights = jnp.exp(jax.random.uniform(jax.random.fold_in(own, dim), (blocks,), jnp.float32, smallest / len(split), high / len(split)))
        gain = gain * jnp.repeat(heights, shape[dim] // blocks).reshape([-1 if axis == dim else 1 for axis in range(len(shape))])
    return gain


def profile(number_of, total, limit, slope):
    loads = [(1 << 20) // math.isqrt(standing ** slope) + 1 for standing in range(2, number_of + 1)]
    rest, counts = total - limit - (number_of - 1), [1] * (number_of - 1)
    while rest > 0:
        candidates = [i for i in range(number_of - 1) if counts[i] < limit]
        whole, remaining = sum([loads[i] for i in candidates]), rest
        for i in candidates:
            more = min(limit - counts[i], max(1, remaining * loads[i] // whole), rest)
            counts[i] = counts[i] + more
            rest = rest - more
    return np.array([limit] + counts)


def ragged_sizes(key, amount, total, reach, skew):
    if amount == 2:
        one = jax.random.randint(key, (), max(1, total - reach), min(reach, total - 1) + 1)
        return jnp.stack([one, total - one])
    tallies = jnp.asarray(profile(amount, total, reach, skew), jnp.int32)
    pairs = (amount - 1) // 2
    source_of, taker = tallies[1:1 + 2 * pairs:2], tallies[2:2 + 2 * pairs:2]
    slack = jnp.minimum(source_of - 1, reach - taker)
    shifted = jax.random.randint(jax.random.fold_in(key, 1), (pairs,), 0, 1 << 20) % (slack + 1)
    tallies = tallies.at[1:1 + 2 * pairs:2].set(source_of - shifted).at[2:2 + 2 * pairs:2].set(taker + shifted)
    return tallies[jax.random.permutation(jax.random.fold_in(key, 2), amount)]


def noise(stream_key, dims, deviation, limit, pieces=(), held_as=jnp.bfloat16):
    array = jax.random.normal(stream_key, dims, jnp.float32) * deviation
    if len(pieces) > 0:
        array = level_of(stream_key, dims, pieces, -0.22, 0.18) * array
    return jnp.clip(array, min=-limit, max=limit).astype(held_as)


def setup_inputs(seed: int = 0) -> dict:
    splits = jax.random.split(jax.random.key(seed), 10)
    queries = draw_queries(jax.random.fold_in(splits[9], 71), 0)
    keys = draw_keys(jax.random.fold_in(splits[9], 71), 0)
    values = noise(splits[2], (PACKED_TOKENS, KEY_VALUE_HEADS * HEAD_SIZE), 1.0, 6.0, ((0, 64), (1, 4)))
    output_gradient = noise(splits[3], (PACKED_TOKENS, QUERY_HEADS * HEAD_SIZE), 1.0, 6.0, ((0, 64), (1, 4)))
    prompt_slot_keys = noise(splits[4], (IMAGE_PROMPTS * PROMPT_LENGTH, KEY_VALUE_HEADS * HEAD_SIZE), 1.0, 6.0, ((0, 64), (1, 4)))
    prompt_slot_values = noise(splits[5], (IMAGE_PROMPTS * PROMPT_LENGTH, KEY_VALUE_HEADS * HEAD_SIZE), 1.0, 6.0, ((0, 64), (1, 4)))
    query_weight = noise(splits[6], (D, QUERY_HEADS * HEAD_SIZE), (QUERY_HEADS * HEAD_SIZE) ** -0.5, 0.078125, ((0, 64), (1, 4)))
    lengths = ragged_sizes(splits[7], RESPONSES, PACKED_TOKENS, TOKENS_PER_SHARD, 2).astype(jnp.int32)
    prompt_owner = jax.random.permutation(splits[8], IMAGE_PROMPTS).astype(jnp.int32)
    return {"queries": queries, "keys": keys, "values": values, "output_gradient": output_gradient, "prompt_slot_keys": prompt_slot_keys, "prompt_slot_values": prompt_slot_values, "query_weight": query_weight, "lengths": lengths, "prompt_owner": prompt_owner}


def labels(lengths):
    rows = jnp.arange(PACKED_TOKENS, dtype=jnp.int32)
    ends = jnp.cumsum(lengths).astype(jnp.int32)
    before = ends[None, :] <= rows[:, None]
    resp = lax.optimization_barrier(jnp.sum(before.astype(jnp.int32), axis=1))
    starts = lax.optimization_barrier(jnp.sum(jnp.where(before, lengths[None, :], 0), axis=1)).astype(jnp.int32)
    return (rows, starts, (resp // RESP_PER).astype(jnp.int32))

def reference(queries, keys, values, output_gradient, prompt_slot_keys, prompt_slot_values, query_weight, lengths, prompt_owner):
    query_group = QUERY_HEADS // KEY_VALUE_HEADS
    scale = 1.0 / math.sqrt(HEAD_SIZE)
    highest = lax.Precision.HIGHEST
    rows, starts, rprompt = labels(lengths)
    prompt_key_count = prompt_slot_keys.shape[0]
    plen = prompt_key_count // IMAGE_PROMPTS
    slots = jnp.arange(prompt_key_count, dtype=jnp.int32) // plen
    kprompt = lax.optimization_barrier(jnp.sum(jnp.where(prompt_owner[None, :] == slots[:, None], jnp.arange(IMAGE_PROMPTS, dtype=jnp.int32)[None, :], 0), axis=1)).astype(jnp.int32)
    prompt_key_rows = prompt_slot_keys.astype(jnp.float32).reshape(prompt_key_count, KEY_VALUE_HEADS, HEAD_SIZE)
    prompt_value_rows = prompt_slot_values.astype(jnp.float32).reshape(prompt_key_count, KEY_VALUE_HEADS, HEAD_SIZE)
    empty_rows = jnp.zeros((TOKENS_PER_SHARD, KEY_VALUE_HEADS * HEAD_SIZE), jnp.float32)
    padded_keys = jnp.concatenate([empty_rows, keys.astype(jnp.float32)], axis=0).reshape(PACKED_TOKENS + TOKENS_PER_SHARD, KEY_VALUE_HEADS, HEAD_SIZE)
    padded_values = jnp.concatenate([empty_rows, values.astype(jnp.float32)], axis=0).reshape(PACKED_TOKENS + TOKENS_PER_SHARD, KEY_VALUE_HEADS, HEAD_SIZE)

    def block(carry, index):
        gpk, gpv, gk, gv = carry
        first_index = (index * TOKENS_PER_SHARD).astype(jnp.int32)
        query_rows = lax.dynamic_slice_in_dim(queries, first_index, TOKENS_PER_SHARD, 0).astype(jnp.float32).reshape(TOKENS_PER_SHARD, KEY_VALUE_HEADS, query_group, HEAD_SIZE)
        gradient_total = lax.dynamic_slice_in_dim(output_gradient, first_index, TOKENS_PER_SHARD, 0).astype(jnp.float32).reshape(TOKENS_PER_SHARD, KEY_VALUE_HEADS, query_group, HEAD_SIZE)
        row_now = lax.dynamic_slice_in_dim(rows, first_index, TOKENS_PER_SHARD, 0)
        start_now = lax.dynamic_slice_in_dim(starts, first_index, TOKENS_PER_SHARD, 0)
        prompt_now = lax.dynamic_slice_in_dim(rprompt, first_index, TOKENS_PER_SHARD, 0)
        wkeys = lax.dynamic_slice_in_dim(padded_keys, first_index, 2 * TOKENS_PER_SHARD, 0)
        wvals = lax.dynamic_slice_in_dim(padded_values, first_index, 2 * TOKENS_PER_SHARD, 0)
        wpos = first_index - TOKENS_PER_SHARD + jnp.arange(2 * TOKENS_PER_SHARD, dtype=jnp.int32)
        allk = jnp.concatenate([prompt_key_rows, wkeys], axis=0)
        allv = jnp.concatenate([prompt_value_rows, wvals], axis=0)
        pmask = prompt_now[:, None] == kprompt[None, :]
        smask = (wpos[None, :] >= start_now[:, None]) & (wpos[None, :] <= row_now[:, None])
        mask = jnp.concatenate([pmask, smask], axis=1)[None, None]
        scores = jnp.einsum('rhgd,khd->hgrk', query_rows, allk, precision=highest) * scale
        high = lax.optimization_barrier(jnp.max(jnp.where(mask, scores, -jnp.inf), axis=-1))
        total = lax.optimization_barrier(jnp.sum(jnp.where(mask, jnp.exp(scores - high[..., None]), 0.0), axis=-1))
        lse = high + jnp.log(total)
        prob = jnp.where(mask, jnp.exp(scores - lse[..., None]), 0.0)
        out = jnp.einsum('hgrk,khd->rhgd', prob, allv, precision=highest)
        delta = jnp.transpose(lax.optimization_barrier(jnp.sum(gradient_total * out, axis=-1)), (1, 2, 0))
        dprob = jnp.einsum('rhgd,khd->hgrk', gradient_total, allv, precision=highest)
        dscore = (prob * (dprob - delta[..., None])).astype(jnp.bfloat16).astype(jnp.float32)
        probw = prob.astype(jnp.bfloat16).astype(jnp.float32)
        dquery = jnp.einsum('hgrk,khd->rhgd', dscore, allk, precision=highest) * scale
        key_gradient = jnp.einsum('hgrk,rhgd->khd', dscore, query_rows, precision=highest) * scale
        value_gradient = jnp.einsum('hgrk,rhgd->khd', probw, gradient_total, precision=highest)
        key_gradient = key_gradient.reshape(prompt_key_count + 2 * TOKENS_PER_SHARD, KEY_VALUE_HEADS * HEAD_SIZE)
        value_gradient = value_gradient.reshape(prompt_key_count + 2 * TOKENS_PER_SHARD, KEY_VALUE_HEADS * HEAD_SIZE)
        gpk = gpk + key_gradient[:prompt_key_count]
        gpv = gpv + value_gradient[:prompt_key_count]
        zero = jnp.zeros((), jnp.int32)
        gk = lax.dynamic_update_slice(gk, lax.dynamic_slice_in_dim(gk, first_index, 2 * TOKENS_PER_SHARD, 0) + key_gradient[prompt_key_count:], (first_index, zero))
        gv = lax.dynamic_update_slice(gv, lax.dynamic_slice_in_dim(gv, first_index, 2 * TOKENS_PER_SHARD, 0) + value_gradient[prompt_key_count:], (first_index, zero))
        return ((gpk, gpv, gk, gv), dquery.reshape(TOKENS_PER_SHARD, QUERY_HEADS * HEAD_SIZE).astype(jnp.bfloat16))
    initial_state = (jnp.zeros((prompt_key_count, KEY_VALUE_HEADS * HEAD_SIZE), jnp.float32), jnp.zeros((prompt_key_count, KEY_VALUE_HEADS * HEAD_SIZE), jnp.float32), jnp.zeros((PACKED_TOKENS + TOKENS_PER_SHARD, KEY_VALUE_HEADS * HEAD_SIZE), jnp.float32), jnp.zeros((PACKED_TOKENS + TOKENS_PER_SHARD, KEY_VALUE_HEADS * HEAD_SIZE), jnp.float32))
    (gpk, gpv, gk, gv), dqs = lax.scan(block, initial_state, jnp.arange(PACKED_TOKENS // TOKENS_PER_SHARD, dtype=jnp.int32))
    grad_queries = dqs.reshape(PACKED_TOKENS, QUERY_HEADS * HEAD_SIZE)
    grad_input = jnp.dot(grad_queries, query_weight.T, preferred_element_type=jnp.float32).astype(jnp.bfloat16)
    return (grad_queries, gk[TOKENS_PER_SHARD:].astype(jnp.bfloat16), gv[TOKENS_PER_SHARD:].astype(jnp.bfloat16), gpk.astype(jnp.bfloat16), gpv.astype(jnp.bfloat16), grad_input)
```

```python
import functools
import math

import jax
import jax.numpy as jnp
from jax import lax
from jax.experimental import pallas as pl
from jax.experimental.pallas import tpu as pltpu
from jax.sharding import PartitionSpec as P

QUERY_HEADS = 40
KEY_VALUE_HEADS = 8
GROUP = QUERY_HEADS // KEY_VALUE_HEADS
HEAD = 128
PROMPTS = 8
RESP_PER = 16
RESPONSES = 128
NZ, NX, NC, NY = 8, 4, 2, 4
TOK = 128
KVH = 2
PROWS = 32
WROWS = 80
QCOLS = KVH * GROUP * HEAD
LANES = GROUP * HEAD
BLK = NZ * WROWS // NY

NEG = -1e30
SCALE = 1.0 / math.sqrt(HEAD)
F32 = jnp.float32
BF = jnp.bfloat16
MESH = pl.DeviceIdType.MESH


def dot(a, b, ca, cb):
    return lax.dot_general(a, b, (((ca,), (cb,)), ((), ())), preferred_element_type=F32)


def kernel(
    near, wide, nsem,
    q_ref, k_ref, v_ref, g_ref, pk_ref, pv_ref, w_ref, lenv_ref, lens_ref, owner_ref,
    gq_ref, gk_ref, gv_ref, gpk_ref, gpv_ref, gi_ref,
    kvz, kvg, wk, wv, wall, gqall, qm, gm, sbuf, dbuf, pbuf, dsbuf, dsm,
    acc, accw, wsend, wrecv, csend, crecv, xown, xsend, xrecv, gsum, zsend, zrecv,
    part, ysend, yrecv, osend, ogi, send_sem, recv_sem,
):
    dp = lax.axis_index("dp")
    y = lax.axis_index("tensor")
    z, x, c = dp // 8, (dp // 2) % 4, dp % 2
    gidx = dp % 8
    oc = 1 - c

    def device(dz=0, dx=0, flip=False, dy=0):
        z2 = lax.rem(z + dz, NZ)
        x2 = lax.rem(x + dx, NX)
        c2 = oc if flip else c
        return (z2 * 8 + x2 * 2 + c2, lax.rem(y + dy, NY))

    nxt = (lax.rem(dp + 1, 64), y)
    prv = (lax.rem(dp + 63, 64), y)
    count = [0]

    def send(src, dst, target):
        i = count[0]
        count[0] = i + 1
        copy = pltpu.make_async_remote_copy(
            src_ref=src, dst_ref=dst, send_sem=send_sem.at[i], recv_sem=recv_sem.at[i],
            device_id=target, device_id_type=MESH,
        )
        copy.start()
        sent.append(copy)
        return copy

    sent = []
    barrier = pltpu.get_barrier_semaphore()
    peers = [device(dz=d) for d in range(1, NZ)]
    peers += [device(dx=d) for d in range(1, NX)]
    peers += [device(flip=True)]
    peers += [device(dy=d) for d in range(1, NY)]
    peers += [nxt, prv]
    for peer in peers:
        pl.semaphore_signal(barrier, inc=1, device_id=peer, device_id_type=MESH)

    kvz[pl.ds(z, 1), :, 0:256] = pk_ref[...][None]
    kvz[pl.ds(z, 1), :, 256:512] = pv_ref[...][None]
    wk[TOK:, :] = k_ref[...]
    wv[TOK:, :] = v_ref[...]
    wall[pl.ds(z, 1)] = w_ref[...][None]

    pl.semaphore_wait(barrier, len(peers))
    zin = [
        send(kvz.at[pl.ds(z, 1)], kvz.at[pl.ds(z, 1)], device(dz=d))
        for d in (4, 3, 5, 2, 6, 1, 7)
    ]
    nin = [
        send(k_ref, wk.at[pl.ds(0, TOK)], nxt),
        send(v_ref, wv.at[pl.ds(0, TOK)], nxt),
    ]

    first = dp * TOK
    ri = lax.broadcasted_iota(jnp.int32, (RESPONSES, RESPONSES), 0)
    ci = lax.broadcasted_iota(jnp.int32, (RESPONSES, RESPONSES), 1)
    len_l = jnp.broadcast_to(lenv_ref[...].astype(F32), (RESPONSES, RESPONSES))
    len_col = jnp.sum(jnp.where(ri == ci, len_l, 0.0), axis=1, keepdims=True)
    ends_col = jnp.sum(jnp.where(ci <= ri, len_l, 0.0), axis=1, keepdims=True)
    len_s = jnp.broadcast_to(len_col, (RESPONSES, RESPONSES))
    ends_row = jnp.sum(jnp.where(ri <= ci, len_s, 0.0), axis=0, keepdims=True)
    rows_l = (first + ci).astype(F32)
    rows_s = (first + ri).astype(F32)
    before_l = ends_col <= rows_l
    before_s = ends_row <= rows_s
    resp_row = jnp.sum(jnp.where(before_l, 1.0, 0.0), axis=0, keepdims=True)
    start_row = jnp.sum(jnp.where(before_l, len_s, 0.0), axis=0, keepdims=True)
    resp_col = jnp.sum(jnp.where(before_s, 1.0, 0.0), axis=1, keepdims=True)
    prompt_row = jnp.floor(resp_row * (1.0 / RESP_PER))
    prompt_col = jnp.floor(resp_col * (1.0 / RESP_PER))
    wpos = (first - TOK + lax.broadcasted_iota(jnp.int32, (2 * TOK, TOK), 0)).astype(F32)
    wmask = (wpos >= start_row) & (wpos <= rows_l[0:1])

    first_group = z * (8 * TOK)

    def walk(r, carry):
        end, ng, nd = carry
        end = end + lens_ref[r]
        ng = ng + jnp.where(end <= first_group, 1, 0)
        nd = nd + jnp.where(end <= first, 1, 0)
        return (end, ng, nd)

    zero = jnp.int32(0)
    _, ng, nd = lax.fori_loop(0, RESPONSES, walk, (zero, zero, zero), unroll=8)
    pg = ng // RESP_PER
    pd = nd // RESP_PER
    slot_of = [owner_ref[jnp.minimum(pg + n, PROMPTS - 1)] for n in range(wide)]
    in_group = [jnp.minimum(pd - pg + n, wide - 1) for n in range(near)]

    mcol = [
        jnp.broadcast_to(jnp.where(prompt_col == (pd + n).astype(F32), 1.0, 0.0), (TOK, HEAD)).astype(BF)
        for n in range(near)
    ]
    mrow = [
        jnp.broadcast_to(jnp.where(prompt_row == (pd + n).astype(F32), 1.0, 0.0), (2 * TOK, TOK)).astype(BF)
        for n in range(near)
    ]
    for h in range(KVH):
        for g in range(GROUP):
            cols = slice((h * GROUP + g) * HEAD, (h * GROUP + g + 1) * HEAD)
            rows = slice(g * HEAD, (g + 1) * HEAD)
            qb = q_ref[:, cols]
            gb = g_ref[:, cols]
            qm[h, rows, near * HEAD:] = qb
            gm[h, rows, near * HEAD:] = gb
            for n in range(near):
                qm[h, rows, n * HEAD:(n + 1) * HEAD] = qb * mcol[n]
                gm[h, rows, n * HEAD:(n + 1) * HEAD] = gb * mcol[n]

    for copy in zin:
        copy.wait_recv()
    for n in range(wide):
        kvg[pl.ds(gidx, 1), n] = kvz[pl.ds(slot_of[n], 1)]
    own = kvg.at[pl.ds(gidx, 1)]
    xin = [send(own, own, device(dx=d)) for d in (1, 3, 2)]
    fin = [send(own, own, device(flip=True))]

    def ring(step):
        up = lax.rem(z + NZ - step, NZ)
        down = lax.rem(z + step, NZ)
        out = [send(wall.at[pl.ds(up, 1)], wall.at[pl.ds(up, 1)], device(dz=1))]
        if step < 3:
            out.append(send(wall.at[pl.ds(down, 1)], wall.at[pl.ds(down, 1)], device(dz=7)))
        return out

    win = ring(0)

    for copy in nin:
        copy.wait_recv()
    for h in range(KVH):
        hc = slice(h * HEAD, (h + 1) * HEAD)
        sbuf[h, 256:, :] = dot(wk[:, hc], qm[h, :, near * HEAD:], 1, 1)
        dbuf[h, 256:, :] = dot(wv[:, hc], gm[h, :, near * HEAD:], 1, 1)

    for d, copy in zip((1, 3, 2), xin):
        copy.wait_recv()
        block = kvg.at[pl.ds(lax.rem(x + NX - d, NX) * 2 + c, 1)]
        fin.append(send(block, block, device(flip=True)))
    for copy in win:
        copy.wait_recv()
    win = ring(1)
    for copy in fin:
        copy.wait_recv()

    def prompt_block(n, lo, width):
        block = kvg[:, pl.ds(in_group[n], 1), :, lo:lo + width]
        return block.reshape(8 * PROWS, width)

    acc[near] = jnp.zeros(acc.shape[1:], F32)
    gin = []
    for h in range(KVH):
        hc = slice(h * HEAD, (h + 1) * HEAD)
        kp = [prompt_block(n, h * HEAD, HEAD) for n in range(near)]
        vp = [prompt_block(n, 256 + h * HEAD, HEAD) for n in range(near)]
        sbuf[h, 0:256, :] = dot(jnp.concatenate(kp, axis=1), qm[h, :, 0:near * HEAD], 1, 1)
        dbuf[h, 0:256, :] = dot(jnp.concatenate(vp, axis=1), gm[h, :, 0:near * HEAD], 1, 1)
        for g in range(GROUP):
            gl = slice(g * HEAD, (g + 1) * HEAD)
            sp = sbuf[h, 0:256, gl] * SCALE
            sw = jnp.where(wmask, sbuf[h, 256:512, gl] * SCALE, NEG)
            high = jnp.maximum(
                jnp.max(sp, axis=0, keepdims=True), jnp.max(sw, axis=0, keepdims=True)
            )
            ep = jnp.exp(sp - high)
            ew = jnp.exp(sw - high)
            total = jnp.sum(ep, axis=0, keepdims=True) + jnp.sum(ew, axis=0, keepdims=True)
            inv = 1.0 / total
            pp = ep * inv
            pw = ew * inv
            dpp = dbuf[h, 0:256, gl]
            dpw = dbuf[h, 256:512, gl]
            delta = jnp.sum(pp * dpp, axis=0, keepdims=True) + jnp.sum(pw * dpw, axis=0, keepdims=True)
            dsp = (pp * (dpp - delta)).astype(BF)
            dsw = (pw * (dpw - delta)).astype(BF)
            pbuf[0:256, gl] = pp.astype(BF)
            pbuf[256:512, gl] = pw.astype(BF)
            dsbuf[:, gl] = dsp
            dsm[near * 256:, gl] = dsw
            for n in range(near):
                dsm[n * 256:(n + 1) * 256, gl] = dsp * mrow[n]
        keys = jnp.concatenate(kp + [wk[:, hc]], axis=0)
        dqt = (dot(keys, dsm[...], 0, 0) * SCALE)
        gqt = dqt.astype(BF)
        for g in range(GROUP):
            head = h * GROUP + g
            gl = slice(g * HEAD, (g + 1) * HEAD)
            gqall[0, 0, head * HEAD:(head + 1) * HEAD, :] = gqt[:, gl]
        half = pl.ds(h * LANES, LANES)
        mine = gqall.at[0, 0, half]
        gin.append(
            [send(mine, gqall.at[d, 0, half], device(dx=d)) for d in (1, 3, 2)]
            + [send(mine, gqall.at[0, 1, half], device(flip=True))]
        )
        for g in range(GROUP):
            head = h * GROUP + g
            gq_ref[:, head * HEAD:(head + 1) * HEAD] = dqt[:, g * HEAD:(g + 1) * HEAD].T.astype(BF)
        dv = dot(pbuf[0:256, :], gm[h, :, 0:near * HEAD], 1, 0)
        dk = dot(dsbuf[...], qm[h, :, 0:near * HEAD], 1, 0) * SCALE
        for n in range(near):
            acc[n, :, hc] = dk[:, n * HEAD:(n + 1) * HEAD]
            acc[n, :, 256 + h * HEAD:256 + (h + 1) * HEAD] = dv[:, n * HEAD:(n + 1) * HEAD]
        accw[0, :, hc] = dot(dsm[near * 256:, :], qm[h, :, near * HEAD:], 1, 0) * SCALE
        accw[1, :, hc] = dot(pbuf[256:512, :], gm[h, :, near * HEAD:], 1, 0)
        for copy in win:
            copy.wait_recv()
        win = ring(2 + h)

    wsend[...] = accw[:, 0:TOK, :].astype(BF)
    back = send(wsend, wrecv, prv)

    held = [
        jnp.where((pg + n - pd >= 0) & (pg + n - pd < near), pg + n - pd, near) for n in range(wide)
    ]

    def term(n, row):
        return acc[pl.ds(held[n], 1), pl.ds(pl.multiple_of(row * PROWS, PROWS), PROWS), :]

    for xs in range(NX):
        for n in range(wide):
            csend[xs, n:n + 1] = term(n, xs * 2 + oc).astype(BF)
    cin = send(csend, crecv, device(flip=True))

    def chunk(d):
        both = jnp.concatenate([gqall[d, 0], gqall[d, 1]], axis=1)
        part[d] = dot(wall[...].reshape(NZ * WROWS, QCOLS), both, 1, 0)
        ysend[d] = part[d].astype(BF)
        out = []
        for e in (2, 1, 3):
            rows = pl.ds(pl.multiple_of(lax.rem(y + e, NY) * BLK, 16), BLK)
            out.append(send(ysend.at[d, rows], yrecv.at[d, e - 1], device(dy=e)))
        return out

    def finish(d, copies):
        for copy in copies:
            copy.wait_recv()
        total = part[d, pl.ds(pl.multiple_of(y * BLK, 16), BLK), :]
        for e in range(3):
            total = total + yrecv[d, e].astype(F32)
        total = total.astype(BF)
        osend[d, 0] = total[:, 0:TOK]
        osend[d, 1] = total[:, TOK:]
        target = lax.rem(x + NX - d, NX)
        out = []
        if d == 0:
            ogi[pl.ds(gidx, 1)] = total[:, 0:TOK][None]
        else:
            out.append(send(osend.at[d, pl.ds(0, 1)], ogi.at[pl.ds(gidx, 1)], (z * 8 + target * 2 + c, y)))
        out.append(send(osend.at[d, pl.ds(1, 1)], ogi.at[pl.ds(gidx, 1)], (z * 8 + target * 2 + oc, y)))
        return out

    for copy in win:
        copy.wait_recv()
    for copies in gin:
        copies[3].wait_recv()
    yin = {0: chunk(0)}

    cin.wait_recv()
    for n in range(wide):
        for xs in range(NX):
            total = term(n, xs * 2 + c) + crecv[xs, n:n + 1].astype(F32)
            xown[xs, n:n + 1] = total
            xsend[xs, n:n + 1] = total.astype(BF)
    rin = [
        send(xsend.at[lax.rem(x + d, NX)], xrecv.at[d - 1], device(dx=d)) for d in (1, 3, 2)
    ]

    oin = []
    forwarded = {}
    for i, d in ((0, 1), (1, 3), (2, 2)):
        forwarded[d] = []
        for h in range(KVH):
            half = pl.ds(h * LANES, LANES)
            gin[h][i].wait_recv()
            forwarded[d].append(send(gqall.at[d, 0, half], gqall.at[d, 1, half], device(flip=True)))
        for copy in forwarded[d]:
            copy.wait_recv()
        yin[d] = chunk(d)
        if d == 1:
            oin += finish(0, yin[0])
        elif d == 3:
            for copy in rin:
                copy.wait_recv()
            for n in range(wide):
                total = xown[pl.ds(x, 1), n:n + 1][0]
                for e in range(3):
                    total = total + xrecv[e, n:n + 1].astype(F32)
                gsum[n:n + 1] = total
            gsum[wide] = jnp.zeros(gsum.shape[1:], F32)

            def pick(target):
                index = jnp.int32(wide)
                for n in range(wide):
                    hit = (slot_of[n] == target) & (pg + n < PROMPTS)
                    index = jnp.where(hit, n, index)
                return gsum[pl.ds(index, 1)]

            gin_z = []
            for dz in (4, 3, 5, 2, 6, 1, 7):
                zsend[dz - 1:dz] = pick(lax.rem(z + dz, NZ)).astype(BF)
                gin_z.append(send(zsend.at[dz - 1], zrecv.at[dz - 1], device(dz=dz)))
            oin += finish(1, yin[1])
        else:
            oin += finish(3, yin[3])
    oin += finish(2, yin[2])

    back.wait_recv()
    gk_ref[...] = (accw[0, TOK:, :] + wrecv[0].astype(F32)).astype(BF)
    gv_ref[...] = (accw[1, TOK:, :] + wrecv[1].astype(F32)).astype(BF)
    for copy in gin_z:
        copy.wait_recv()
    total = pick(z)[0]
    for e in range(NZ - 1):
        total = total + zrecv[e].astype(F32)
    gpk_ref[...] = total[:, 0:256].astype(BF)
    gpv_ref[...] = total[:, 256:512].astype(BF)

    for copy in oin:
        copy.wait_recv()
    blocks = []
    for zz in range(2):
        for j in range(8):
            blocks.append(ogi[j, zz * WROWS:(zz + 1) * WROWS, :])
    git = jnp.concatenate(blocks, axis=0)
    for i in range(QCOLS // HEAD):
        gi_ref[:, i * HEAD:(i + 1) * HEAD] = git[i * HEAD:(i + 1) * HEAD, :].astype(F32).T.astype(BF)
    for copy in sent:
        copy.wait_send()
    assert count[0] <= nsem


def fused(near, wide, cid, queries, keys, values, output_gradient, pk, pv, weight, lengths, owner):
    nsem = 72
    vm = pl.BlockSpec(memory_space=pltpu.VMEM)
    sm = pl.BlockSpec(memory_space=pltpu.SMEM)
    shape = jax.ShapeDtypeStruct
    scratch = [
        pltpu.VMEM((NZ, PROWS, 512), BF),
        pltpu.VMEM((8, wide, PROWS, 512), BF),
        pltpu.VMEM((2 * TOK, 256), BF),
        pltpu.VMEM((2 * TOK, 256), BF),
        pltpu.VMEM((NZ, WROWS, QCOLS), BF),
        pltpu.VMEM((NX, 2, QCOLS, TOK), BF),
        pltpu.VMEM((KVH, LANES, (near + 1) * HEAD), BF),
        pltpu.VMEM((KVH, LANES, (near + 1) * HEAD), BF),
        pltpu.VMEM((KVH, 512, LANES), F32),
        pltpu.VMEM((KVH, 512, LANES), F32),
        pltpu.VMEM((512, LANES), BF),
        pltpu.VMEM((256, LANES), BF),
        pltpu.VMEM(((near + 1) * 256, LANES), BF),
        pltpu.VMEM((near + 1, 256, 512), F32),
        pltpu.VMEM((2, 2 * TOK, 256), F32),
        pltpu.VMEM((2, TOK, 256), BF),
        pltpu.VMEM((2, TOK, 256), BF),
        pltpu.VMEM((NX, wide, PROWS, 512), BF),
        pltpu.VMEM((NX, wide, PROWS, 512), BF),
        pltpu.VMEM((NX, wide, PROWS, 512), F32),
        pltpu.VMEM((NX, wide, PROWS, 512), BF),
        pltpu.VMEM((NX - 1, wide, PROWS, 512), BF),
        pltpu.VMEM((wide + 1, PROWS, 512), F32),
        pltpu.VMEM((NZ - 1, PROWS, 512), BF),
        pltpu.VMEM((NZ - 1, PROWS, 512), BF),
        pltpu.VMEM((NX, NZ * WROWS, 2 * TOK), F32),
        pltpu.VMEM((NX, NZ * WROWS, 2 * TOK), BF),
        pltpu.VMEM((NX, NY - 1, BLK, 2 * TOK), BF),
        pltpu.VMEM((NX, 2, BLK, TOK), BF),
        pltpu.VMEM((8, BLK, TOK), BF),
        pltpu.SemaphoreType.DMA((nsem,)),
        pltpu.SemaphoreType.DMA((nsem,)),
    ]
    return pl.pallas_call(
        functools.partial(kernel, near, wide, nsem),
        out_shape=(
            shape((TOK, QCOLS), BF),
            shape((TOK, 256), BF),
            shape((TOK, 256), BF),
            shape((PROWS, 256), BF),
            shape((PROWS, 256), BF),
            shape((TOK, QCOLS), BF),
        ),
        in_specs=[vm] * 8 + [sm] * 2,
        out_specs=(vm,) * 6,
        scratch_shapes=scratch,
        compiler_params=pltpu.CompilerParams(
            collective_id=cid, has_side_effects=True, vmem_limit_bytes=56 * 2**20
        ),
    )(
        queries, keys, values, output_gradient, pk, pv, weight,
        lengths.reshape(1, RESPONSES), lengths, owner,
    )


NEARWIDE = (6, 6)


def shards(*args):
    return fused(*NEARWIDE, 0, *args)


def solution(mesh):
    split = P("dp", "tensor")
    return jax.shard_map(
        shards,
        mesh=mesh,
        in_specs=(split,) * 7 + (P(), P()),
        out_specs=(split,) * 6,
        check_vma=False,
    )
```

```python
import functools
import math

import jax
import jax.numpy as jnp
from jax import lax
from jax.experimental import pallas as pl
from jax.experimental.pallas import tpu as pltpu
from jax.sharding import PartitionSpec as P

QUERY_HEADS = 40
KEY_VALUE_HEADS = 8
GROUP = QUERY_HEADS // KEY_VALUE_HEADS
HEAD = 128
PROMPTS = 8
RESP_PER = 16
RESPONSES = 128
NZ, NX, NC, NY = 8, 4, 2, 4
TOK = 128
KVH = 2
PROWS = 32
WROWS = 80
QCOLS = KVH * GROUP * HEAD
LANES = GROUP * HEAD
BLK = NZ * WROWS // NY

NEG = -1e30
SCALE = 1.0 / math.sqrt(HEAD)
F32 = jnp.float32
BF = jnp.bfloat16
MESH = pl.DeviceIdType.MESH


def dot(a, b, ca, cb):
    return lax.dot_general(a, b, (((ca,), (cb,)), ((), ())), preferred_element_type=F32)


def kernel(
    near, wide, nsem,
    q_hbm, k_hbm, v_hbm, g_hbm, pk_hbm, pv_hbm, w_hbm, lenv_ref, lens_ref, owner_ref,
    gq_hbm, gk_hbm, gv_hbm, gpk_hbm, gpv_hbm, gi_hbm,
    q_ref, g_ref, gq_ref, gk_ref, gv_ref, gpk_ref, gpv_ref, gi_ref,
    kz, vz, kg, vg, wk, wv, wall, gqall, qm, gm, sbuf, dbuf, pbuf, dsbuf, dsm,
    acc, accw, wsend, wrecv, csend, crecv, xown, xsend, xrecv, gsum, zsend, zrecv,
    part, ysend, ycomb, yrecv, osend, ogi, send_sem, recv_sem, local_sem,
):
    dp = lax.axis_index("dp")
    y = lax.axis_index("tensor")
    z, x, c = dp // 8, (dp // 2) % 4, dp % 2
    gidx = dp % 8
    oc = 1 - c

    def device(dz=0, dx=0, flip=False, dy=0):
        z2 = lax.rem(z + dz, NZ)
        x2 = lax.rem(x + dx, NX)
        c2 = oc if flip else c
        return (z2 * 8 + x2 * 2 + c2, lax.rem(y + dy, NY))

    nxt = (lax.rem(dp + 1, 64), y)
    prv = (lax.rem(dp + 63, 64), y)
    count = [0]
    sent = []
    stores = []

    def send(src, dst, target):
        i = count[0]
        count[0] = i + 1
        copy = pltpu.make_async_remote_copy(
            src_ref=src, dst_ref=dst, send_sem=send_sem.at[i], recv_sem=recv_sem.at[i],
            device_id=target, device_id_type=MESH,
        )
        copy.start()
        sent.append(copy)
        return copy

    def store(src, dst):
        copy = pltpu.make_async_copy(src, dst, local_sem.at[7 + len(stores)])
        copy.start()
        stores.append(copy)

    def arrive(copies):
        for copy in copies:
            copy.wait_recv()

    barrier = pltpu.get_barrier_semaphore()
    peers = [device(dz=d) for d in range(1, NZ)]
    peers += [device(dx=d) for d in range(1, NX)]
    peers += [device(flip=True)]
    peers += [device(dy=d) for d in range(1, NY)]
    peers += [nxt, prv]
    for peer in peers:
        pl.semaphore_signal(barrier, inc=1, device_id=peer, device_id_type=MESH)

    loads = [
        pltpu.make_async_copy(src, dst, local_sem.at[i])
        for i, (src, dst) in enumerate([
            (pk_hbm, kz.at[z]),
            (pv_hbm, vz.at[z]),
            (k_hbm, wk.at[pl.ds(TOK, TOK)]),
            (v_hbm, wv.at[pl.ds(TOK, TOK)]),
            (w_hbm, wall.at[z]),
            (q_hbm, q_ref),
            (g_hbm, g_ref),
        ])
    ]
    for load in loads:
        load.start()
    for load in loads[:4]:
        load.wait()
    pl.semaphore_wait(barrier, len(peers))
    far = (4, 3, 5, 2, 6, 1, 7)
    zk_in = [send(kz.at[z], kz.at[z], device(dz=d)) for d in far]
    zv_in = [send(vz.at[z], vz.at[z], device(dz=d)) for d in far]
    near_in = [
        send(wk.at[pl.ds(TOK, TOK)], wk.at[pl.ds(0, TOK)], nxt),
        send(wv.at[pl.ds(TOK, TOK)], wv.at[pl.ds(0, TOK)], nxt),
    ]

    first = dp * TOK
    ri = lax.broadcasted_iota(jnp.int32, (RESPONSES, RESPONSES), 0)
    ci = lax.broadcasted_iota(jnp.int32, (RESPONSES, RESPONSES), 1)
    len_l = jnp.broadcast_to(lenv_ref[...].astype(F32), (RESPONSES, RESPONSES))
    len_col = jnp.sum(jnp.where(ri == ci, len_l, 0.0), axis=1, keepdims=True)
    ends_col = jnp.sum(jnp.where(ci <= ri, len_l, 0.0), axis=1, keepdims=True)
    len_s = jnp.broadcast_to(len_col, (RESPONSES, RESPONSES))
    ends_row = jnp.sum(jnp.where(ri <= ci, len_s, 0.0), axis=0, keepdims=True)
    rows_l = (first + ci).astype(F32)
    rows_s = (first + ri).astype(F32)
    before_l = ends_col <= rows_l
    before_s = ends_row <= rows_s
    resp_row = jnp.sum(jnp.where(before_l, 1.0, 0.0), axis=0, keepdims=True)
    start_row = jnp.sum(jnp.where(before_l, len_s, 0.0), axis=0, keepdims=True)
    resp_col = jnp.sum(jnp.where(before_s, 1.0, 0.0), axis=1, keepdims=True)
    prompt_row = jnp.floor(resp_row * (1.0 / RESP_PER))
    prompt_col = jnp.floor(resp_col * (1.0 / RESP_PER))
    wpos = (first - TOK + lax.broadcasted_iota(jnp.int32, (2 * TOK, TOK), 0)).astype(F32)
    wmask = (wpos >= start_row) & (wpos <= rows_l[0:1])

    first_group = z * (8 * TOK)

    def walk(r, carry):
        end, ng, nd = carry
        end = end + lens_ref[r]
        ng = ng + jnp.where(end <= first_group, 1, 0)
        nd = nd + jnp.where(end <= first, 1, 0)
        return (end, ng, nd)

    zero = jnp.int32(0)
    _, ng, nd = lax.fori_loop(0, RESPONSES, walk, (zero, zero, zero), unroll=8)
    pg = ng // RESP_PER
    pd = nd // RESP_PER
    slot_of = [owner_ref[jnp.minimum(pg + n, PROMPTS - 1)] for n in range(wide)]
    in_group = [jnp.minimum(pd - pg + n, wide - 1) for n in range(near)]
    held = [
        jnp.where((pg + n - pd >= 0) & (pg + n - pd < near), pg + n - pd, near) for n in range(wide)
    ]

    mcol = [
        jnp.broadcast_to(jnp.where(prompt_col == (pd + n).astype(F32), 1.0, 0.0), (TOK, HEAD)).astype(BF)
        for n in range(near)
    ]
    mrow = [
        jnp.broadcast_to(jnp.where(prompt_row == (pd + n).astype(F32), 1.0, 0.0), (2 * TOK, TOK)).astype(BF)
        for n in range(near)
    ]
    for load in loads[4:]:
        load.wait()
    for h in range(KVH):
        for g in range(GROUP):
            cols = slice((h * GROUP + g) * HEAD, (h * GROUP + g + 1) * HEAD)
            rows = slice(g * HEAD, (g + 1) * HEAD)
            qb = q_ref[:, cols]
            gb = g_ref[:, cols]
            qm[h, rows, near * HEAD:] = qb
            gm[h, rows, near * HEAD:] = gb
            for n in range(near):
                qm[h, rows, n * HEAD:(n + 1) * HEAD] = qb * mcol[n]
                gm[h, rows, n * HEAD:(n + 1) * HEAD] = gb * mcol[n]

    def spread(source, dest):
        for n in range(wide):
            dest[pl.ds(gidx, 1), n] = source[pl.ds(slot_of[n], 1)]
        own = dest.at[pl.ds(gidx, 1)]
        across = [send(own, own, device(dx=d)) for d in (1, 3, 2)]
        return across, [send(own, own, device(flip=True))]

    def collect(dest, across, flips):
        for d, copy in zip((1, 3, 2), across):
            copy.wait_recv()
            block = dest.at[pl.ds(lax.rem(x + NX - d, NX) * 2 + c, 1)]
            flips.append(send(block, block, device(flip=True)))
        arrive(flips)

    arrive(zk_in)
    kx_in, kf_in = spread(kz, kg)
    arrive(zv_in)
    vx_in, vf_in = spread(vz, vg)

    pieces = (pl.ds(0, 48), pl.ds(48, 32))

    def ring(step, piece):
        up = wall.at[lax.rem(z + NZ - step, NZ), pieces[piece]]
        down = wall.at[lax.rem(z + step, NZ), pieces[piece]]
        if step == 3:
            return [send(up, up, device(dz=1))] if piece == 0 else [send(down, down, device(dz=7))]
        return [send(up, up, device(dz=1)), send(down, down, device(dz=7))]

    ring_in = {}

    def advance(step, piece):
        if step > 0:
            arrive(ring_in[step - 1, piece])
        ring_in[step, piece] = ring(step, piece)

    advance(0, 0)
    advance(0, 1)

    arrive(near_in)
    for h in range(KVH):
        hc = slice(h * HEAD, (h + 1) * HEAD)
        sbuf[h, 256:, :] = dot(wk[:, hc], qm[h, :, near * HEAD:], 1, 1)
        dbuf[h, 256:, :] = dot(wv[:, hc], gm[h, :, near * HEAD:], 1, 1)

    def prompt_block(source, n, h):
        block = source[:, pl.ds(in_group[n], 1), :, h * HEAD:(h + 1) * HEAD]
        return block.reshape(8 * PROWS, HEAD)

    collect(kg, kx_in, kf_in)
    kp = [[prompt_block(kg, n, h) for n in range(near)] for h in range(KVH)]
    for h in range(KVH):
        sbuf[h, 0:256, :] = dot(jnp.concatenate(kp[h], axis=1), qm[h, :, 0:near * HEAD], 1, 1)
    collect(vg, vx_in, vf_in)
    advance(1, 0)

    acc[near] = jnp.zeros(acc.shape[1:], F32)

    def softmax(h):
        vp = [prompt_block(vg, n, h) for n in range(near)]
        dbuf[h, 0:256, :] = dot(jnp.concatenate(vp, axis=1), gm[h, :, 0:near * HEAD], 1, 1)
        for g in range(GROUP):
            gl = slice(g * HEAD, (g + 1) * HEAD)
            sp = sbuf[h, 0:256, gl] * SCALE
            sw = jnp.where(wmask, sbuf[h, 256:512, gl] * SCALE, NEG)
            high = jnp.maximum(
                jnp.max(sp, axis=0, keepdims=True), jnp.max(sw, axis=0, keepdims=True)
            )
            ep = jnp.exp(sp - high)
            ew = jnp.exp(sw - high)
            total = jnp.sum(ep, axis=0, keepdims=True) + jnp.sum(ew, axis=0, keepdims=True)
            inv = 1.0 / total
            pp = ep * inv
            pw = ew * inv
            dpp = dbuf[h, 0:256, gl]
            dpw = dbuf[h, 256:512, gl]
            delta = jnp.sum(pp * dpp, axis=0, keepdims=True) + jnp.sum(pw * dpw, axis=0, keepdims=True)
            dsp = (pp * (dpp - delta)).astype(BF)
            dsw = (pw * (dpw - delta)).astype(BF)
            pbuf[0:256, gl] = pp.astype(BF)
            pbuf[256:512, gl] = pw.astype(BF)
            dsbuf[:, gl] = dsp
            dsm[near * 256:, gl] = dsw
            for n in range(near):
                dsm[n * 256:(n + 1) * 256, gl] = dsp * mrow[n]

    halves = [pl.ds(h * LANES, LANES) for h in range(KVH)]

    def query_grad(h):
        hc = slice(h * HEAD, (h + 1) * HEAD)
        keys = jnp.concatenate(kp[h] + [wk[:, hc]], axis=0)
        dqt = dot(keys, dsm[...], 0, 0) * SCALE
        gqt = dqt.astype(BF)
        for g in range(GROUP):
            head = h * GROUP + g
            gqall[0, 0, head * HEAD:(head + 1) * HEAD, :] = gqt[:, g * HEAD:(g + 1) * HEAD]
        mine = gqall.at[0, 0, halves[h]]
        copies = {d: send(mine, gqall.at[d, 0, halves[h]], device(dx=d)) for d in (1, 3)}
        copies[0] = send(mine, gqall.at[0, 1, halves[h]], device(flip=True))
        for g in range(GROUP):
            head = h * GROUP + g
            gq_ref[:, head * HEAD:(head + 1) * HEAD] = dqt[:, g * HEAD:(g + 1) * HEAD].T.astype(BF)
        return copies

    def pass_on(h, copies):
        out = []
        for d, lo in ((1, h * LANES), (3, h * LANES + LANES // 2)):
            copies[d].wait_recv()
            rows = pl.ds(lo, LANES // 2)
            out.append(send(gqall.at[d, 0, rows], gqall.at[2, 0, rows], device(dx=d)))
        flips = {
            d: send(gqall.at[d, 0, halves[h]], gqall.at[d, 1, halves[h]], device(flip=True))
            for d in (1, 3)
        }
        return out, flips

    def key_grad(h):
        hc = slice(h * HEAD, (h + 1) * HEAD)
        dv = dot(pbuf[0:256, :], gm[h, :, 0:near * HEAD], 1, 0)
        dk = dot(dsbuf[...], qm[h, :, 0:near * HEAD], 1, 0) * SCALE
        for n in range(near):
            acc[n, h, :, 0:HEAD] = dk[:, n * HEAD:(n + 1) * HEAD]
            acc[n, h, :, HEAD:] = dv[:, n * HEAD:(n + 1) * HEAD]
        for xs in range(NX):
            for n in range(wide):
                csend[h, xs, n] = term(h, n, xs * 2 + oc).astype(BF)
        copy = send(csend.at[h], crecv.at[h], device(flip=True))
        accw[0, :, hc] = dot(dsm[near * 256:, :], qm[h, :, near * HEAD:], 1, 0) * SCALE
        accw[1, :, hc] = dot(pbuf[256:512, :], gm[h, :, near * HEAD:], 1, 0)
        return copy

    def term(h, n, row):
        rows = pl.ds(pl.multiple_of(row * PROWS, PROWS), PROWS)
        return acc[pl.ds(held[n], 1), h, rows, :][0]

    def over_x(h, copy):
        copy.wait_recv()
        for n in range(wide):
            for xs in range(NX):
                total = term(h, n, xs * 2 + c) + crecv[h, xs, n].astype(F32)
                xown[h, xs, n] = total
                xsend[h, xs, n] = total.astype(BF)
        return [
            send(xsend.at[h, lax.rem(x + d, NX)], xrecv.at[h, d - 1], device(dx=d)) for d in (1, 3, 2)
        ]

    def pick(h, target):
        index = jnp.int32(wide)
        for n in range(wide):
            hit = (slot_of[n] == target) & (pg + n < PROMPTS)
            index = jnp.where(hit, n, index)
        return gsum[h, pl.ds(index, 1)][0]

    def over_z(h, copies):
        arrive(copies)
        for n in range(wide):
            total = xown[h, pl.ds(x, 1), n][0]
            for e in range(3):
                total = total + xrecv[h, e, n].astype(F32)
            gsum[h, n] = total
        gsum[h, wide] = jnp.zeros(gsum.shape[2:], F32)
        out = []
        for dz in far:
            zsend[h, dz - 1] = pick(h, lax.rem(z + dz, NZ)).astype(BF)
            out.append(send(zsend.at[h, dz - 1], zrecv.at[h, dz - 1], device(dz=dz)))
        return out

    def yrows(e):
        return pl.ds(pl.multiple_of(lax.rem(y + e, NY) * BLK, 16), BLK)

    def chunk(d):
        both = jnp.concatenate([gqall[d, 0], gqall[d, 1]], axis=1)
        out = dot(wall[...].reshape(NZ * WROWS, QCOLS), both, 1, 0)
        for e in range(2):
            part[d, e] = out[:, e * TOK:(e + 1) * TOK]
            ysend[d, e] = out[:, e * TOK:(e + 1) * TOK].astype(BF)
        up, down = device(dy=1), device(dy=3)
        return [
            send(ysend.at[d, 0, yrows(2)], yrecv.at[d, 0], up),
            send(ysend.at[d, 1, yrows(2)], yrecv.at[d, 1], down),
            send(ysend.at[d, 1, yrows(1)], yrecv.at[d, 2], up),
            send(ysend.at[d, 0, yrows(3)], yrecv.at[d, 3], down),
        ]

    def relay(d, copies):
        copies[0].wait_recv()
        ycomb[d, 0] = (part[d, 0, yrows(1), :] + yrecv[d, 0].astype(F32)).astype(BF)
        copies.append(send(ycomb.at[d, 0], yrecv.at[d, 4], device(dy=1)))
        copies[1].wait_recv()
        ycomb[d, 1] = (part[d, 1, yrows(3), :] + yrecv[d, 1].astype(F32)).astype(BF)
        copies.append(send(ycomb.at[d, 1], yrecv.at[d, 5], device(dy=3)))

    def finish(d, copies):
        arrive(copies[2:])
        own = yrows(0)
        owner_x = lax.rem(x + NX - d, NX)
        out = []
        for e, (a, b) in enumerate(((4, 3), (2, 5))):
            total = part[d, e, own, :] + yrecv[d, a].astype(F32) + yrecv[d, b].astype(F32)
            if d == 0 and e == 0:
                ogi[pl.ds(gidx, 1)] = total.astype(BF)[None]
            else:
                osend[d, e] = total.astype(BF)
                target = (z * 8 + owner_x * 2 + (oc if e else c), y)
                out.append(send(osend.at[d, e], ogi.at[gidx], target))
        return out

    softmax(0)
    gin0 = query_grad(0)
    advance(1, 1)
    c_in0 = key_grad(0)
    softmax(1)
    gin1 = query_grad(1)
    advance(2, 0)
    c_in1 = key_grad(1)
    wsend[...] = accw[:, 0:TOK, :].astype(BF)
    back = send(wsend, wrecv, prv)
    advance(2, 1)
    gx0, gf0 = pass_on(0, gin0)
    store(gq_ref, gq_hbm)
    x_in0 = over_x(0, c_in0)
    advance(3, 0)
    advance(3, 1)
    gx1, gf1 = pass_on(1, gin1)
    x_in1 = over_x(1, c_in1)
    arrive([gin0[0], gin1[0]])
    arrive(ring_in[3, 0] + ring_in[3, 1])
    y0 = chunk(0)
    arrive([gf0[1], gf1[1]])
    y1 = chunk(1)
    arrive([gf0[3], gf1[3]])
    y3 = chunk(3)
    arrive(gx0 + gx1)
    opposite = send(gqall.at[2, 0], gqall.at[2, 1], device(flip=True))
    relay(0, y0)
    arrive([opposite])
    y2 = chunk(2)
    relay(1, y1)
    relay(3, y3)
    z_in0 = over_z(0, x_in0)
    relay(2, y2)
    z_in1 = over_z(1, x_in1)
    o_in = finish(0, y0)
    o_in += finish(1, y1)
    o_in += finish(3, y3)

    back.wait_recv()
    gk_ref[...] = (accw[0, TOK:, :] + wrecv[0].astype(F32)).astype(BF)
    gv_ref[...] = (accw[1, TOK:, :] + wrecv[1].astype(F32)).astype(BF)
    store(gk_ref, gk_hbm)
    store(gv_ref, gv_hbm)
    o_in += finish(2, y2)

    arrive(z_in0 + z_in1)
    for h in range(KVH):
        total = pick(h, z)
        for e in range(NZ - 1):
            total = total + zrecv[h, e].astype(F32)
        gpk_ref[:, h * HEAD:(h + 1) * HEAD] = total[:, 0:HEAD].astype(BF)
        gpv_ref[:, h * HEAD:(h + 1) * HEAD] = total[:, HEAD:].astype(BF)
    store(gpk_ref, gpk_hbm)
    store(gpv_ref, gpv_hbm)

    arrive(o_in)
    blocks = []
    for zz in range(2):
        for j in range(8):
            blocks.append(ogi[j, zz * WROWS:(zz + 1) * WROWS, :])
    git = jnp.concatenate(blocks, axis=0)
    for i in range(QCOLS // HEAD):
        gi_ref[:, i * HEAD:(i + 1) * HEAD] = git[i * HEAD:(i + 1) * HEAD, :].astype(F32).T.astype(BF)
    store(gi_ref, gi_hbm)
    for copy in sent:
        copy.wait_send()
    for copy in stores:
        copy.wait()
    assert count[0] <= nsem


def settle_kernel(count, *refs):
    held = refs[2 * count:3 * count]
    sem = refs[-1]
    inward = [pltpu.make_async_copy(refs[i], held[i], sem.at[0, i]) for i in range(count)]
    for copy in inward:
        copy.start()
    outward = [
        pltpu.make_async_copy(held[i], refs[count + i], sem.at[1, i]) for i in range(count)
    ]
    for i in range(count):
        inward[i].wait()
        outward[i].start()
    for copy in outward:
        copy.wait()


def settle(arrays):
    hb = pl.BlockSpec(memory_space=pl.ANY)
    count = len(arrays)
    return pl.pallas_call(
        functools.partial(settle_kernel, count),
        out_shape=tuple(jax.ShapeDtypeStruct(a.shape, a.dtype) for a in arrays),
        in_specs=[hb] * count,
        out_specs=(hb,) * count,
        scratch_shapes=[pltpu.VMEM(a.shape, a.dtype) for a in arrays]
        + [pltpu.SemaphoreType.DMA((2, count))],
        compiler_params=pltpu.CompilerParams(vmem_limit_bytes=56 * 2**20),
    )(*arrays)


def fused(near, wide, cid, queries, keys, values, output_gradient, pk, pv, weight, lengths, owner):
    nsem = 120
    vm = pl.BlockSpec(memory_space=pltpu.VMEM)
    sm = pl.BlockSpec(memory_space=pltpu.SMEM)
    hb = pl.BlockSpec(memory_space=pl.ANY)
    shape = jax.ShapeDtypeStruct
    results = [(TOK, QCOLS), (TOK, 256), (TOK, 256), (PROWS, 256), (PROWS, 256), (TOK, QCOLS)]
    scratch = [pltpu.VMEM((TOK, QCOLS), BF), pltpu.VMEM((TOK, QCOLS), BF)]
    scratch += [pltpu.VMEM(r, BF) for r in results]
    scratch += [
        pltpu.VMEM((NZ, PROWS, 256), BF),
        pltpu.VMEM((NZ, PROWS, 256), BF),
        pltpu.VMEM((8, wide, PROWS, 256), BF),
        pltpu.VMEM((8, wide, PROWS, 256), BF),
        pltpu.VMEM((2 * TOK, 256), BF),
        pltpu.VMEM((2 * TOK, 256), BF),
        pltpu.VMEM((NZ, WROWS, QCOLS), BF),
        pltpu.VMEM((NX, 2, QCOLS, TOK), BF),
        pltpu.VMEM((KVH, LANES, (near + 1) * HEAD), BF),
        pltpu.VMEM((KVH, LANES, (near + 1) * HEAD), BF),
        pltpu.VMEM((KVH, 512, LANES), F32),
        pltpu.VMEM((KVH, 512, LANES), F32),
        pltpu.VMEM((512, LANES), BF),
        pltpu.VMEM((256, LANES), BF),
        pltpu.VMEM(((near + 1) * 256, LANES), BF),
        pltpu.VMEM((near + 1, KVH, 256, 256), F32),
        pltpu.VMEM((2, 2 * TOK, 256), F32),
        pltpu.VMEM((2, TOK, 256), BF),
        pltpu.VMEM((2, TOK, 256), BF),
        pltpu.VMEM((KVH, NX, wide, PROWS, 256), BF),
        pltpu.VMEM((KVH, NX, wide, PROWS, 256), BF),
        pltpu.VMEM((KVH, NX, wide, PROWS, 256), F32),
        pltpu.VMEM((KVH, NX, wide, PROWS, 256), BF),
        pltpu.VMEM((KVH, NX - 1, wide, PROWS, 256), BF),
        pltpu.VMEM((KVH, wide + 1, PROWS, 256), F32),
        pltpu.VMEM((KVH, NZ - 1, PROWS, 256), BF),
        pltpu.VMEM((KVH, NZ - 1, PROWS, 256), BF),
        pltpu.VMEM((NX, 2, NZ * WROWS, TOK), F32),
        pltpu.VMEM((NX, 2, NZ * WROWS, TOK), BF),
        pltpu.VMEM((NX, 2, BLK, TOK), BF),
        pltpu.VMEM((NX, 6, BLK, TOK), BF),
        pltpu.VMEM((NX, 2, BLK, TOK), BF),
        pltpu.VMEM((8, BLK, TOK), BF),
        pltpu.SemaphoreType.DMA((nsem,)),
        pltpu.SemaphoreType.DMA((nsem,)),
        pltpu.SemaphoreType.DMA((13,)),
    ]
    results = pl.pallas_call(
        functools.partial(kernel, near, wide, nsem),
        out_shape=tuple(shape(r, BF) for r in results),
        in_specs=[hb] * 7 + [vm] + [sm] * 2,
        out_specs=(hb,) * 6,
        scratch_shapes=scratch,
        compiler_params=pltpu.CompilerParams(
            collective_id=cid, has_side_effects=True, vmem_limit_bytes=56 * 2**20
        ),
    )(
        queries, keys, values, output_gradient, pk, pv, weight,
        lengths.reshape(1, RESPONSES), lengths, owner,
    )
    return settle(results)


def few_prompts(lengths):
    tokens = jnp.sum(lengths.reshape(PROMPTS, RESP_PER), axis=1)
    return jnp.min(tokens) >= 4 * TOK


def shards(*args):
    return lax.cond(
        few_prompts(args[7]),
        functools.partial(fused, 2, 3, 0),
        functools.partial(fused, 6, 6, 1),
        *args,
    )


def solution(mesh):
    split = P("dp", "tensor")
    return jax.shard_map(
        shards,
        mesh=mesh,
        in_specs=(split,) * 7 + (P(), P()),
        out_specs=(split,) * 6,
        check_vma=False,
    )
```

```python
import functools
import math

import jax
import jax.numpy as jnp
from jax import lax
from jax.experimental import pallas as pl
from jax.experimental.pallas import tpu as pltpu
from jax.sharding import PartitionSpec as P

QUERY_HEADS = 40
KEY_VALUE_HEADS = 8
GROUP = QUERY_HEADS // KEY_VALUE_HEADS
HEAD = 128
PROMPTS = 8
RESP_PER = 16
RESPONSES = 128
NZ, NX, NC, NY = 8, 4, 2, 4
TOK = 128
KVH = 2
PROWS = 32
WROWS = 80
QCOLS = KVH * GROUP * HEAD
LANES = GROUP * HEAD
BLK = NZ * WROWS // NY

NEG = -1e30
SCALE = 1.0 / math.sqrt(HEAD)
F32 = jnp.float32
BF = jnp.bfloat16
MESH = pl.DeviceIdType.MESH


def dot(a, b, ca, cb):
    return lax.dot_general(a, b, (((ca,), (cb,)), ((), ())), preferred_element_type=F32)


def kernel(
    near, wide, nsem,
    q_hbm, k_hbm, v_hbm, g_hbm, pk_hbm, pv_hbm, w_hbm, lenv_ref, lens_ref, owner_ref,
    gq_hbm, gk_hbm, gv_hbm, gpk_hbm, gpv_hbm, gi_hbm,
    q_ref, g_ref, gq_ref, gk_ref, gv_ref, gpk_ref, gpv_ref, gi_ref,
    kz, vz, kg, vg, wk, wv, wall, gqall, qm, gm, sbuf, dbuf, pbuf, dsbuf, dsm,
    acc, accw, wsend, wrecv, csend, crecv, xown, xsend, xrecv, gsum, zsend, zrecv,
    part, ysend, ycomb, yrecv, osend, ogi, send_sem, recv_sem, local_sem,
):
    dp = lax.axis_index("dp")
    y = lax.axis_index("tensor")
    z, x, c = dp // 8, (dp // 2) % 4, dp % 2
    gidx = dp % 8
    oc = 1 - c

    def device(dz=0, dx=0, flip=False, dy=0):
        z2 = lax.rem(z + dz, NZ)
        x2 = lax.rem(x + dx, NX)
        c2 = oc if flip else c
        return (z2 * 8 + x2 * 2 + c2, lax.rem(y + dy, NY))

    nxt = (lax.rem(dp + 1, 64), y)
    prv = (lax.rem(dp + 63, 64), y)
    count = [0]
    sent = []
    stores = []

    def send(src, dst, target):
        i = count[0]
        count[0] = i + 1
        copy = pltpu.make_async_remote_copy(
            src_ref=src, dst_ref=dst, send_sem=send_sem.at[i], recv_sem=recv_sem.at[i],
            device_id=target, device_id_type=MESH,
        )
        copy.start()
        sent.append(copy)
        return copy

    def store(src, dst):
        copy = pltpu.make_async_copy(src, dst, local_sem.at[7 + len(stores)])
        copy.start()
        stores.append(copy)

    def arrive(copies):
        for copy in copies:
            copy.wait_recv()

    barrier = pltpu.get_barrier_semaphore()
    peers = [device(dz=d) for d in range(1, NZ)]
    peers += [device(dx=d) for d in range(1, NX)]
    peers += [device(flip=True)]
    peers += [device(dy=d) for d in range(1, NY)]
    peers += [nxt, prv]
    for peer in peers:
        pl.semaphore_signal(barrier, inc=1, device_id=peer, device_id_type=MESH)

    loads = [
        pltpu.make_async_copy(src, dst, local_sem.at[i])
        for i, (src, dst) in enumerate([
            (pk_hbm, kz.at[z]),
            (pv_hbm, vz.at[z]),
            (k_hbm, wk.at[pl.ds(TOK, TOK)]),
            (v_hbm, wv.at[pl.ds(TOK, TOK)]),
            (w_hbm, wall.at[z]),
            (q_hbm, q_ref),
            (g_hbm, g_ref),
        ])
    ]
    for load in loads:
        load.start()
    for load in loads[:4]:
        load.wait()
    pl.semaphore_wait(barrier, len(peers))
    far = (4, 3, 5, 2, 6, 1, 7)
    zk_in = [send(kz.at[z], kz.at[z], device(dz=d)) for d in far]
    zv_in = [send(vz.at[z], vz.at[z], device(dz=d)) for d in far]
    near_in = [
        send(wk.at[pl.ds(TOK, TOK)], wk.at[pl.ds(0, TOK)], nxt),
        send(wv.at[pl.ds(TOK, TOK)], wv.at[pl.ds(0, TOK)], nxt),
    ]

    first = dp * TOK
    ri = lax.broadcasted_iota(jnp.int32, (RESPONSES, RESPONSES), 0)
    ci = lax.broadcasted_iota(jnp.int32, (RESPONSES, RESPONSES), 1)
    len_l = jnp.broadcast_to(lenv_ref[...].astype(F32), (RESPONSES, RESPONSES))
    len_col = jnp.sum(jnp.where(ri == ci, len_l, 0.0), axis=1, keepdims=True)
    ends_col = jnp.sum(jnp.where(ci <= ri, len_l, 0.0), axis=1, keepdims=True)
    len_s = jnp.broadcast_to(len_col, (RESPONSES, RESPONSES))
    ends_row = jnp.sum(jnp.where(ri <= ci, len_s, 0.0), axis=0, keepdims=True)
    rows_l = (first + ci).astype(F32)
    rows_s = (first + ri).astype(F32)
    before_l = ends_col <= rows_l
    before_s = ends_row <= rows_s
    resp_row = jnp.sum(jnp.where(before_l, 1.0, 0.0), axis=0, keepdims=True)
    start_row = jnp.sum(jnp.where(before_l, len_s, 0.0), axis=0, keepdims=True)
    resp_col = jnp.sum(jnp.where(before_s, 1.0, 0.0), axis=1, keepdims=True)
    prompt_row = jnp.floor(resp_row * (1.0 / RESP_PER))
    prompt_col = jnp.floor(resp_col * (1.0 / RESP_PER))
    wpos = (first - TOK + lax.broadcasted_iota(jnp.int32, (2 * TOK, TOK), 0)).astype(F32)
    wmask = (wpos >= start_row) & (wpos <= rows_l[0:1])

    first_group = z * (8 * TOK)

    def walk(r, carry):
        end, ng, nd = carry
        end = end + lens_ref[r]
        ng = ng + jnp.where(end <= first_group, 1, 0)
        nd = nd + jnp.where(end <= first, 1, 0)
        return (end, ng, nd)

    zero = jnp.int32(0)
    _, ng, nd = lax.fori_loop(0, RESPONSES, walk, (zero, zero, zero), unroll=8)
    pg = ng // RESP_PER
    pd = nd // RESP_PER
    slot_of = [owner_ref[jnp.minimum(pg + n, PROMPTS - 1)] for n in range(wide)]
    in_group = [jnp.minimum(pd - pg + n, wide - 1) for n in range(near)]
    held = [
        jnp.where((pg + n - pd >= 0) & (pg + n - pd < near), pg + n - pd, near) for n in range(wide)
    ]

    mcol = [
        jnp.broadcast_to(jnp.where(prompt_col == (pd + n).astype(F32), 1.0, 0.0), (TOK, HEAD)).astype(BF)
        for n in range(near)
    ]
    mrow = [
        jnp.broadcast_to(jnp.where(prompt_row == (pd + n).astype(F32), 1.0, 0.0), (2 * TOK, TOK)).astype(BF)
        for n in range(near)
    ]
    for load in loads[4:]:
        load.wait()
    for h in range(KVH):
        for g in range(GROUP):
            cols = slice((h * GROUP + g) * HEAD, (h * GROUP + g + 1) * HEAD)
            rows = slice(g * HEAD, (g + 1) * HEAD)
            qb = q_ref[:, cols]
            gb = g_ref[:, cols]
            qm[h, rows, near * HEAD:] = qb
            gm[h, rows, near * HEAD:] = gb
            for n in range(near):
                qm[h, rows, n * HEAD:(n + 1) * HEAD] = qb * mcol[n]
                gm[h, rows, n * HEAD:(n + 1) * HEAD] = gb * mcol[n]

    def spread(source, dest):
        for n in range(wide):
            dest[pl.ds(gidx, 1), n] = source[pl.ds(slot_of[n], 1)]
        own = dest.at[pl.ds(gidx, 1)]
        across = [send(own, own, device(dx=d)) for d in (1, 3, 2)]
        return across, [send(own, own, device(flip=True))]

    def collect(dest, across, flips):
        for d, copy in zip((1, 3, 2), across):
            copy.wait_recv()
            block = dest.at[pl.ds(lax.rem(x + NX - d, NX) * 2 + c, 1)]
            flips.append(send(block, block, device(flip=True)))
        arrive(flips)

    arrive(zk_in)
    kx_in, kf_in = spread(kz, kg)
    arrive(zv_in)
    vx_in, vf_in = spread(vz, vg)

    pieces = (pl.ds(0, 48), pl.ds(48, 32))

    def ring(step, piece):
        up = wall.at[lax.rem(z + NZ - step, NZ), pieces[piece]]
        down = wall.at[lax.rem(z + step, NZ), pieces[piece]]
        if step == 3:
            return [send(up, up, device(dz=1))] if piece == 0 else [send(down, down, device(dz=7))]
        return [send(up, up, device(dz=1)), send(down, down, device(dz=7))]

    ring_in = {}

    def advance(step, piece):
        if step > 0:
            arrive(ring_in[step - 1, piece])
        ring_in[step, piece] = ring(step, piece)

    advance(0, 0)
    advance(0, 1)

    arrive(near_in)
    for h in range(KVH):
        hc = slice(h * HEAD, (h + 1) * HEAD)
        sbuf[h, 256:, :] = dot(wk[:, hc], qm[h, :, near * HEAD:], 1, 1)
        dbuf[h, 256:, :] = dot(wv[:, hc], gm[h, :, near * HEAD:], 1, 1)

    def prompt_block(source, n, h):
        block = source[:, pl.ds(in_group[n], 1), :, h * HEAD:(h + 1) * HEAD]
        return block.reshape(8 * PROWS, HEAD)

    collect(kg, kx_in, kf_in)
    kp = [[prompt_block(kg, n, h) for n in range(near)] for h in range(KVH)]
    for h in range(KVH):
        sbuf[h, 0:256, :] = dot(jnp.concatenate(kp[h], axis=1), qm[h, :, 0:near * HEAD], 1, 1)
    collect(vg, vx_in, vf_in)
    advance(1, 0)

    acc[near] = jnp.zeros(acc.shape[1:], F32)

    def softmax(h):
        vp = [prompt_block(vg, n, h) for n in range(near)]
        dbuf[h, 0:256, :] = dot(jnp.concatenate(vp, axis=1), gm[h, :, 0:near * HEAD], 1, 1)
        for g in range(GROUP):
            gl = slice(g * HEAD, (g + 1) * HEAD)
            sp = sbuf[h, 0:256, gl] * SCALE
            sw = jnp.where(wmask, sbuf[h, 256:512, gl] * SCALE, NEG)
            high = jnp.maximum(
                jnp.max(sp, axis=0, keepdims=True), jnp.max(sw, axis=0, keepdims=True)
            )
            ep = jnp.exp(sp - high)
            ew = jnp.exp(sw - high)
            total = jnp.sum(ep, axis=0, keepdims=True) + jnp.sum(ew, axis=0, keepdims=True)
            inv = 1.0 / total
            pp = ep * inv
            pw = ew * inv
            dpp = dbuf[h, 0:256, gl]
            dpw = dbuf[h, 256:512, gl]
            delta = jnp.sum(pp * dpp, axis=0, keepdims=True) + jnp.sum(pw * dpw, axis=0, keepdims=True)
            dsp = (pp * (dpp - delta)).astype(BF)
            dsw = (pw * (dpw - delta)).astype(BF)
            pbuf[0:256, gl] = pp.astype(BF)
            pbuf[256:512, gl] = pw.astype(BF)
            dsbuf[:, gl] = dsp
            dsm[near * 256:, gl] = dsw
            for n in range(near):
                dsm[n * 256:(n + 1) * 256, gl] = dsp * mrow[n]

    halves = [pl.ds(h * LANES, LANES) for h in range(KVH)]

    def query_grad(h):
        hc = slice(h * HEAD, (h + 1) * HEAD)
        keys = jnp.concatenate(kp[h] + [wk[:, hc]], axis=0)
        dqt = dot(keys, dsm[...], 0, 0) * SCALE
        gqt = dqt.astype(BF)
        for g in range(GROUP):
            head = h * GROUP + g
            gqall[0, 0, head * HEAD:(head + 1) * HEAD, :] = gqt[:, g * HEAD:(g + 1) * HEAD]
        mine = gqall.at[0, 0, halves[h]]
        copies = {d: send(mine, gqall.at[d, 0, halves[h]], device(dx=d)) for d in (1, 3)}
        copies[0] = send(mine, gqall.at[0, 1, halves[h]], device(flip=True))
        for g in range(GROUP):
            head = h * GROUP + g
            gq_ref[:, head * HEAD:(head + 1) * HEAD] = dqt[:, g * HEAD:(g + 1) * HEAD].T.astype(BF)
        return copies

    def pass_on(h, copies):
        out = []
        for d, lo in ((1, h * LANES), (3, h * LANES + LANES // 2)):
            copies[d].wait_recv()
            rows = pl.ds(lo, LANES // 2)
            out.append(send(gqall.at[d, 0, rows], gqall.at[2, 0, rows], device(dx=d)))
        flips = {
            d: send(gqall.at[d, 0, halves[h]], gqall.at[d, 1, halves[h]], device(flip=True))
            for d in (1, 3)
        }
        return out, flips

    def key_grad(h):
        hc = slice(h * HEAD, (h + 1) * HEAD)
        dv = dot(pbuf[0:256, :], gm[h, :, 0:near * HEAD], 1, 0)
        dk = dot(dsbuf[...], qm[h, :, 0:near * HEAD], 1, 0) * SCALE
        for n in range(near):
            acc[n, h, :, 0:HEAD] = dk[:, n * HEAD:(n + 1) * HEAD]
            acc[n, h, :, HEAD:] = dv[:, n * HEAD:(n + 1) * HEAD]
        for xs in range(NX):
            for n in range(wide):
                csend[h, xs, n] = term(h, n, xs * 2 + oc).astype(BF)
        copy = send(csend.at[h], crecv.at[h], device(flip=True))
        accw[0, :, hc] = dot(dsm[near * 256:, :], qm[h, :, near * HEAD:], 1, 0) * SCALE
        accw[1, :, hc] = dot(pbuf[256:512, :], gm[h, :, near * HEAD:], 1, 0)
        return copy

    def term(h, n, row):
        rows = pl.ds(pl.multiple_of(row * PROWS, PROWS), PROWS)
        return acc[pl.ds(held[n], 1), h, rows, :][0]

    def over_x(h, copy):
        copy.wait_recv()
        for n in range(wide):
            for xs in range(NX):
                total = term(h, n, xs * 2 + c) + crecv[h, xs, n].astype(F32)
                xown[h, xs, n] = total
                xsend[h, xs, n] = total.astype(BF)
        return [
            send(xsend.at[h, lax.rem(x + d, NX)], xrecv.at[h, d - 1], device(dx=d)) for d in (1, 3, 2)
        ]

    def pick(h, target):
        index = jnp.int32(wide)
        for n in range(wide):
            hit = (slot_of[n] == target) & (pg + n < PROMPTS)
            index = jnp.where(hit, n, index)
        return gsum[h, pl.ds(index, 1)][0]

    def over_z(h, copies):
        arrive(copies)
        for n in range(wide):
            total = xown[h, pl.ds(x, 1), n][0]
            for e in range(3):
                total = total + xrecv[h, e, n].astype(F32)
            gsum[h, n] = total
        gsum[h, wide] = jnp.zeros(gsum.shape[2:], F32)
        out = []
        for dz in far:
            zsend[h, dz - 1] = pick(h, lax.rem(z + dz, NZ)).astype(BF)
            out.append(send(zsend.at[h, dz - 1], zrecv.at[h, dz - 1], device(dz=dz)))
        return out

    def yrows(e):
        return pl.ds(pl.multiple_of(lax.rem(y + e, NY) * BLK, 16), BLK)

    def chunk(d):
        both = jnp.concatenate([gqall[d, 0], gqall[d, 1]], axis=1)
        out = dot(wall[...].reshape(NZ * WROWS, QCOLS), both, 1, 0)
        for e in range(2):
            part[d, e] = out[:, e * TOK:(e + 1) * TOK]
            ysend[d, e] = out[:, e * TOK:(e + 1) * TOK].astype(BF)
        up, down = device(dy=1), device(dy=3)
        return [
            send(ysend.at[d, 0, yrows(2)], yrecv.at[d, 0], up),
            send(ysend.at[d, 1, yrows(2)], yrecv.at[d, 1], down),
            send(ysend.at[d, 1, yrows(1)], yrecv.at[d, 2], up),
            send(ysend.at[d, 0, yrows(3)], yrecv.at[d, 3], down),
        ]

    def relay(d, copies):
        copies[0].wait_recv()
        ycomb[d, 0] = (part[d, 0, yrows(1), :] + yrecv[d, 0].astype(F32)).astype(BF)
        copies.append(send(ycomb.at[d, 0], yrecv.at[d, 4], device(dy=1)))
        copies[1].wait_recv()
        ycomb[d, 1] = (part[d, 1, yrows(3), :] + yrecv[d, 1].astype(F32)).astype(BF)
        copies.append(send(ycomb.at[d, 1], yrecv.at[d, 5], device(dy=3)))

    def finish(d, copies):
        arrive(copies[2:])
        own = yrows(0)
        owner_x = lax.rem(x + NX - d, NX)
        out = []
        for e, (a, b) in enumerate(((4, 3), (2, 5))):
            total = part[d, e, own, :] + yrecv[d, a].astype(F32) + yrecv[d, b].astype(F32)
            if d == 0 and e == 0:
                ogi[pl.ds(gidx, 1)] = total.astype(BF)[None]
            else:
                osend[d, e] = total.astype(BF)
                target = (z * 8 + owner_x * 2 + (oc if e else c), y)
                out.append(send(osend.at[d, e], ogi.at[gidx], target))
        return out

    softmax(0)
    gin0 = query_grad(0)
    advance(1, 1)
    c_in0 = key_grad(0)
    softmax(1)
    gin1 = query_grad(1)
    advance(2, 0)
    c_in1 = key_grad(1)
    wsend[...] = accw[:, 0:TOK, :].astype(BF)
    back = send(wsend, wrecv, prv)
    advance(2, 1)
    gx0, gf0 = pass_on(0, gin0)
    store(gq_ref, gq_hbm)
    advance(3, 0)
    advance(3, 1)
    gx1, gf1 = pass_on(1, gin1)
    arrive([gin0[0], gin1[0]])
    arrive(ring_in[3, 0] + ring_in[3, 1])
    x_in0 = over_x(0, c_in0)
    x_in1 = over_x(1, c_in1)
    y0 = chunk(0)
    arrive([gf0[1], gf1[1]])
    y1 = chunk(1)
    arrive([gf0[3], gf1[3]])
    y3 = chunk(3)
    arrive(gx0 + gx1)
    opposite = send(gqall.at[2, 0], gqall.at[2, 1], device(flip=True))
    relay(0, y0)
    arrive([opposite])
    y2 = chunk(2)
    relay(1, y1)
    relay(3, y3)
    z_in0 = over_z(0, x_in0)
    relay(2, y2)
    z_in1 = over_z(1, x_in1)
    o_in = finish(0, y0)
    o_in += finish(1, y1)
    o_in += finish(3, y3)

    back.wait_recv()
    gk_ref[...] = (accw[0, TOK:, :] + wrecv[0].astype(F32)).astype(BF)
    gv_ref[...] = (accw[1, TOK:, :] + wrecv[1].astype(F32)).astype(BF)
    store(gk_ref, gk_hbm)
    store(gv_ref, gv_hbm)
    o_in += finish(2, y2)

    arrive(z_in0 + z_in1)
    for h in range(KVH):
        total = pick(h, z)
        for e in range(NZ - 1):
            total = total + zrecv[h, e].astype(F32)
        gpk_ref[:, h * HEAD:(h + 1) * HEAD] = total[:, 0:HEAD].astype(BF)
        gpv_ref[:, h * HEAD:(h + 1) * HEAD] = total[:, HEAD:].astype(BF)
    store(gpk_ref, gpk_hbm)
    store(gpv_ref, gpv_hbm)

    arrive(o_in)
    blocks = []
    for zz in range(2):
        for j in range(8):
            blocks.append(ogi[j, zz * WROWS:(zz + 1) * WROWS, :])
    git = jnp.concatenate(blocks, axis=0)
    for i in range(QCOLS // HEAD):
        gi_ref[:, i * HEAD:(i + 1) * HEAD] = git[i * HEAD:(i + 1) * HEAD, :].astype(F32).T.astype(BF)
    store(gi_ref, gi_hbm)
    for copy in sent:
        copy.wait_send()
    for copy in stores:
        copy.wait()
    assert count[0] <= nsem


def settle_kernel(count, *refs):
    held = refs[2 * count:3 * count]
    sem = refs[-1]
    inward = [pltpu.make_async_copy(refs[i], held[i], sem.at[0, i]) for i in range(count)]
    for copy in inward:
        copy.start()
    outward = [
        pltpu.make_async_copy(held[i], refs[count + i], sem.at[1, i]) for i in range(count)
    ]
    for i in range(count):
        inward[i].wait()
        outward[i].start()
    for copy in outward:
        copy.wait()


def settle(arrays):
    hb = pl.BlockSpec(memory_space=pl.ANY)
    count = len(arrays)
    return pl.pallas_call(
        functools.partial(settle_kernel, count),
        out_shape=tuple(jax.ShapeDtypeStruct(a.shape, a.dtype) for a in arrays),
        in_specs=[hb] * count,
        out_specs=(hb,) * count,
        scratch_shapes=[pltpu.VMEM(a.shape, a.dtype) for a in arrays]
        + [pltpu.SemaphoreType.DMA((2, count))],
        compiler_params=pltpu.CompilerParams(vmem_limit_bytes=56 * 2**20),
    )(*arrays)


def fused(near, wide, cid, queries, keys, values, output_gradient, pk, pv, weight, lengths, owner):
    nsem = 120
    vm = pl.BlockSpec(memory_space=pltpu.VMEM)
    sm = pl.BlockSpec(memory_space=pltpu.SMEM)
    hb = pl.BlockSpec(memory_space=pl.ANY)
    shape = jax.ShapeDtypeStruct
    results = [(TOK, QCOLS), (TOK, 256), (TOK, 256), (PROWS, 256), (PROWS, 256), (TOK, QCOLS)]
    scratch = [pltpu.VMEM((TOK, QCOLS), BF), pltpu.VMEM((TOK, QCOLS), BF)]
    scratch += [pltpu.VMEM(r, BF) for r in results]
    scratch += [
        pltpu.VMEM((NZ, PROWS, 256), BF),
        pltpu.VMEM((NZ, PROWS, 256), BF),
        pltpu.VMEM((8, wide, PROWS, 256), BF),
        pltpu.VMEM((8, wide, PROWS, 256), BF),
        pltpu.VMEM((2 * TOK, 256), BF),
        pltpu.VMEM((2 * TOK, 256), BF),
        pltpu.VMEM((NZ, WROWS, QCOLS), BF),
        pltpu.VMEM((NX, 2, QCOLS, TOK), BF),
        pltpu.VMEM((KVH, LANES, (near + 1) * HEAD), BF),
        pltpu.VMEM((KVH, LANES, (near + 1) * HEAD), BF),
        pltpu.VMEM((KVH, 512, LANES), F32),
        pltpu.VMEM((KVH, 512, LANES), F32),
        pltpu.VMEM((512, LANES), BF),
        pltpu.VMEM((256, LANES), BF),
        pltpu.VMEM(((near + 1) * 256, LANES), BF),
        pltpu.VMEM((near + 1, KVH, 256, 256), F32),
        pltpu.VMEM((2, 2 * TOK, 256), F32),
        pltpu.VMEM((2, TOK, 256), BF),
        pltpu.VMEM((2, TOK, 256), BF),
        pltpu.VMEM((KVH, NX, wide, PROWS, 256), BF),
        pltpu.VMEM((KVH, NX, wide, PROWS, 256), BF),
        pltpu.VMEM((KVH, NX, wide, PROWS, 256), F32),
        pltpu.VMEM((KVH, NX, wide, PROWS, 256), BF),
        pltpu.VMEM((KVH, NX - 1, wide, PROWS, 256), BF),
        pltpu.VMEM((KVH, wide + 1, PROWS, 256), F32),
        pltpu.VMEM((KVH, NZ - 1, PROWS, 256), BF),
        pltpu.VMEM((KVH, NZ - 1, PROWS, 256), BF),
        pltpu.VMEM((NX, 2, NZ * WROWS, TOK), F32),
        pltpu.VMEM((NX, 2, NZ * WROWS, TOK), BF),
        pltpu.VMEM((NX, 2, BLK, TOK), BF),
        pltpu.VMEM((NX, 6, BLK, TOK), BF),
        pltpu.VMEM((NX, 2, BLK, TOK), BF),
        pltpu.VMEM((8, BLK, TOK), BF),
        pltpu.SemaphoreType.DMA((nsem,)),
        pltpu.SemaphoreType.DMA((nsem,)),
        pltpu.SemaphoreType.DMA((13,)),
    ]
    results = pl.pallas_call(
        functools.partial(kernel, near, wide, nsem),
        out_shape=tuple(shape(r, BF) for r in results),
        in_specs=[hb] * 7 + [vm] + [sm] * 2,
        out_specs=(hb,) * 6,
        scratch_shapes=scratch,
        compiler_params=pltpu.CompilerParams(
            collective_id=cid, has_side_effects=True, vmem_limit_bytes=56 * 2**20
        ),
    )(
        queries, keys, values, output_gradient, pk, pv, weight,
        lengths.reshape(1, RESPONSES), lengths, owner,
    )
    return settle(results)


def few_prompts(lengths):
    tokens = jnp.sum(lengths.reshape(PROMPTS, RESP_PER), axis=1)
    return jnp.min(tokens) >= 4 * TOK


def shards(*args):
    return lax.cond(
        few_prompts(args[7]),
        functools.partial(fused, 2, 3, 0),
        functools.partial(fused, 6, 6, 1),
        *args,
    )


def solution(mesh):
    split = P("dp", "tensor")
    return jax.shard_map(
        shards,
        mesh=mesh,
        in_specs=(split,) * 7 + (P(), P()),
        out_specs=(split,) * 6,
        check_vma=False,
    )
```

```python
import functools
import math

import jax
import jax.numpy as jnp
from jax import lax
from jax.experimental import pallas as pl
from jax.experimental.pallas import tpu as pltpu
from jax.sharding import PartitionSpec as P

QUERY_HEADS = 40
KEY_VALUE_HEADS = 8
GROUP = QUERY_HEADS // KEY_VALUE_HEADS
HEAD = 128
PROMPTS = 8
RESP_PER = 16
RESPONSES = 128
NZ, NX, NC, NY = 8, 4, 2, 4
TOK = 128
KVH = 2
PROWS = 32
WROWS = 80
QCOLS = KVH * GROUP * HEAD
LANES = GROUP * HEAD
BLK = NZ * WROWS // NY

NEG = -1e30
SCALE = 1.0 / math.sqrt(HEAD)
F32 = jnp.float32
BF = jnp.bfloat16
MESH = pl.DeviceIdType.MESH


def dot(a, b, ca, cb):
    return lax.dot_general(a, b, (((ca,), (cb,)), ((), ())), preferred_element_type=F32)


def kernel(
    near, wide, nsem,
    q_hbm, k_hbm, v_hbm, g_hbm, pk_hbm, pv_hbm, w_hbm, lenv_ref, lens_ref, owner_ref,
    gq_hbm, gk_hbm, gv_hbm, gpk_hbm, gpv_hbm, gi_hbm,
    q_ref, g_ref, gq_ref, gk_ref, gv_ref, gpk_ref, gpv_ref, gi_ref,
    kz, vz, kg, vg, wk, wv, wall, gqall, qm, gm, sbuf, dbuf, pbuf, dsbuf, dsm,
    acc, accw, wsend, wrecv, csend, crecv, xown, xsend, xrecv, gsum, zsend, zrecv,
    part, ysend, ycomb, yrecv, osend, ogi, send_sem, recv_sem, local_sem,
):
    dp = lax.axis_index("dp")
    y = lax.axis_index("tensor")
    z, x, c = dp // 8, (dp // 2) % 4, dp % 2
    gidx = dp % 8
    oc = 1 - c

    def device(dz=0, dx=0, flip=False, dy=0):
        z2 = lax.rem(z + dz, NZ)
        x2 = lax.rem(x + dx, NX)
        c2 = oc if flip else c
        return (z2 * 8 + x2 * 2 + c2, lax.rem(y + dy, NY))

    nxt = (lax.rem(dp + 1, 64), y)
    prv = (lax.rem(dp + 63, 64), y)
    count = [0]
    sent = []
    stores = []

    def send(src, dst, target):
        i = count[0]
        count[0] = i + 1
        copy = pltpu.make_async_remote_copy(
            src_ref=src, dst_ref=dst, send_sem=send_sem.at[i], recv_sem=recv_sem.at[i],
            device_id=target, device_id_type=MESH,
        )
        copy.start()
        sent.append(copy)
        return copy

    def store(src, dst):
        copy = pltpu.make_async_copy(src, dst, local_sem.at[7 + len(stores)])
        copy.start()
        stores.append(copy)

    def arrive(copies):
        for copy in copies:
            copy.wait_recv()

    barrier = pltpu.get_barrier_semaphore()
    peers = [device(dz=d) for d in range(1, NZ)]
    peers += [device(dx=d) for d in range(1, NX)]
    peers += [device(flip=True)]
    peers += [device(dy=d) for d in range(1, NY)]
    peers += [nxt, prv]
    for peer in peers:
        pl.semaphore_signal(barrier, inc=1, device_id=peer, device_id_type=MESH)

    loads = [
        pltpu.make_async_copy(src, dst, local_sem.at[i])
        for i, (src, dst) in enumerate([
            (pk_hbm, kz.at[z]),
            (pv_hbm, vz.at[z]),
            (k_hbm, wk.at[pl.ds(TOK, TOK)]),
            (v_hbm, wv.at[pl.ds(TOK, TOK)]),
            (w_hbm, wall.at[z]),
            (q_hbm, q_ref),
            (g_hbm, g_ref),
        ])
    ]
    for load in loads:
        load.start()
    for load in loads[:4]:
        load.wait()
    pl.semaphore_wait(barrier, len(peers))
    far = (4, 3, 5, 2, 6, 1, 7)
    zk_in = [send(kz.at[z], kz.at[z], device(dz=d)) for d in far]
    zv_in = [send(vz.at[z], vz.at[z], device(dz=d)) for d in far]
    near_in = [
        send(wk.at[pl.ds(TOK, TOK)], wk.at[pl.ds(0, TOK)], nxt),
        send(wv.at[pl.ds(TOK, TOK)], wv.at[pl.ds(0, TOK)], nxt),
    ]

    first = dp * TOK
    ri = lax.broadcasted_iota(jnp.int32, (RESPONSES, RESPONSES), 0)
    ci = lax.broadcasted_iota(jnp.int32, (RESPONSES, RESPONSES), 1)
    len_l = jnp.broadcast_to(lenv_ref[...].astype(F32), (RESPONSES, RESPONSES))
    len_col = jnp.sum(jnp.where(ri == ci, len_l, 0.0), axis=1, keepdims=True)
    ends_col = jnp.sum(jnp.where(ci <= ri, len_l, 0.0), axis=1, keepdims=True)
    len_s = jnp.broadcast_to(len_col, (RESPONSES, RESPONSES))
    ends_row = jnp.sum(jnp.where(ri <= ci, len_s, 0.0), axis=0, keepdims=True)
    rows_l = (first + ci).astype(F32)
    rows_s = (first + ri).astype(F32)
    before_l = ends_col <= rows_l
    before_s = ends_row <= rows_s
    resp_row = jnp.sum(jnp.where(before_l, 1.0, 0.0), axis=0, keepdims=True)
    start_row = jnp.sum(jnp.where(before_l, len_s, 0.0), axis=0, keepdims=True)
    resp_col = jnp.sum(jnp.where(before_s, 1.0, 0.0), axis=1, keepdims=True)
    prompt_row = jnp.floor(resp_row * (1.0 / RESP_PER))
    prompt_col = jnp.floor(resp_col * (1.0 / RESP_PER))
    wpos = (first - TOK + lax.broadcasted_iota(jnp.int32, (2 * TOK, TOK), 0)).astype(F32)
    wmask = (wpos >= start_row) & (wpos <= rows_l[0:1])

    first_group = z * (8 * TOK)

    def walk(r, carry):
        end, ng, nd = carry
        end = end + lens_ref[r]
        ng = ng + jnp.where(end <= first_group, 1, 0)
        nd = nd + jnp.where(end <= first, 1, 0)
        return (end, ng, nd)

    zero = jnp.int32(0)
    _, ng, nd = lax.fori_loop(0, RESPONSES, walk, (zero, zero, zero), unroll=8)
    pg = ng // RESP_PER
    pd = nd // RESP_PER
    slot_of = [owner_ref[jnp.minimum(pg + n, PROMPTS - 1)] for n in range(wide)]
    in_group = [jnp.minimum(pd - pg + n, wide - 1) for n in range(near)]
    held = [
        jnp.where((pg + n - pd >= 0) & (pg + n - pd < near), pg + n - pd, near) for n in range(wide)
    ]

    mcol = [
        jnp.broadcast_to(jnp.where(prompt_col == (pd + n).astype(F32), 1.0, 0.0), (TOK, HEAD)).astype(BF)
        for n in range(near)
    ]
    mrow = [
        jnp.broadcast_to(jnp.where(prompt_row == (pd + n).astype(F32), 1.0, 0.0), (2 * TOK, TOK)).astype(BF)
        for n in range(near)
    ]
    for load in loads[4:]:
        load.wait()
    for h in range(KVH):
        for g in range(GROUP):
            cols = slice((h * GROUP + g) * HEAD, (h * GROUP + g + 1) * HEAD)
            rows = slice(g * HEAD, (g + 1) * HEAD)
            qb = q_ref[:, cols]
            gb = g_ref[:, cols]
            qm[h, rows, near * HEAD:] = qb
            gm[h, rows, near * HEAD:] = gb
            for n in range(near):
                qm[h, rows, n * HEAD:(n + 1) * HEAD] = qb * mcol[n]
                gm[h, rows, n * HEAD:(n + 1) * HEAD] = gb * mcol[n]

    def spread(source, dest):
        for n in range(wide):
            dest[pl.ds(gidx, 1), n] = source[pl.ds(slot_of[n], 1)]
        own = dest.at[pl.ds(gidx, 1)]
        across = [send(own, own, device(dx=d)) for d in (1, 3, 2)]
        return across, [send(own, own, device(flip=True))]

    def collect(dest, across, flips):
        for d, copy in zip((1, 3, 2), across):
            copy.wait_recv()
            block = dest.at[pl.ds(lax.rem(x + NX - d, NX) * 2 + c, 1)]
            flips.append(send(block, block, device(flip=True)))
        arrive(flips)

    arrive(zk_in)
    kx_in, kf_in = spread(kz, kg)
    arrive(zv_in)
    vx_in, vf_in = spread(vz, vg)

    pieces = (pl.ds(0, 48), pl.ds(48, 32))

    def ring(step, piece):
        up = wall.at[lax.rem(z + NZ - step, NZ), pieces[piece]]
        down = wall.at[lax.rem(z + step, NZ), pieces[piece]]
        if step == 3:
            return [send(up, up, device(dz=1))] if piece == 0 else [send(down, down, device(dz=7))]
        return [send(up, up, device(dz=1)), send(down, down, device(dz=7))]

    ring_in = {}

    def advance(step, piece):
        if step > 0:
            arrive(ring_in[step - 1, piece])
        ring_in[step, piece] = ring(step, piece)

    advance(0, 0)
    advance(0, 1)

    arrive(near_in)
    for h in range(KVH):
        hc = slice(h * HEAD, (h + 1) * HEAD)
        sbuf[h, 256:, :] = dot(wk[:, hc], qm[h, :, near * HEAD:], 1, 1)
        dbuf[h, 256:, :] = dot(wv[:, hc], gm[h, :, near * HEAD:], 1, 1)

    def prompt_block(source, n, h):
        block = source[:, pl.ds(in_group[n], 1), :, h * HEAD:(h + 1) * HEAD]
        return block.reshape(8 * PROWS, HEAD)

    collect(kg, kx_in, kf_in)
    kp = [[prompt_block(kg, n, h) for n in range(near)] for h in range(KVH)]
    for h in range(KVH):
        sbuf[h, 0:256, :] = dot(jnp.concatenate(kp[h], axis=1), qm[h, :, 0:near * HEAD], 1, 1)
    collect(vg, vx_in, vf_in)
    advance(1, 0)

    acc[near] = jnp.zeros(acc.shape[1:], F32)

    def softmax(h):
        vp = [prompt_block(vg, n, h) for n in range(near)]
        dbuf[h, 0:256, :] = dot(jnp.concatenate(vp, axis=1), gm[h, :, 0:near * HEAD], 1, 1)
        for g in range(GROUP):
            gl = slice(g * HEAD, (g + 1) * HEAD)
            sp = sbuf[h, 0:256, gl] * SCALE
            sw = jnp.where(wmask, sbuf[h, 256:512, gl] * SCALE, NEG)
            high = jnp.maximum(
                jnp.max(sp, axis=0, keepdims=True), jnp.max(sw, axis=0, keepdims=True)
            )
            ep = jnp.exp(sp - high)
            ew = jnp.exp(sw - high)
            total = jnp.sum(ep, axis=0, keepdims=True) + jnp.sum(ew, axis=0, keepdims=True)
            inv = 1.0 / total
            pp = ep * inv
            pw = ew * inv
            dpp = dbuf[h, 0:256, gl]
            dpw = dbuf[h, 256:512, gl]
            delta = jnp.sum(pp * dpp, axis=0, keepdims=True) + jnp.sum(pw * dpw, axis=0, keepdims=True)
            dsp = (pp * (dpp - delta)).astype(BF)
            dsw = (pw * (dpw - delta)).astype(BF)
            pbuf[0:256, gl] = pp.astype(BF)
            pbuf[256:512, gl] = pw.astype(BF)
            dsbuf[:, gl] = dsp
            dsm[near * 256:, gl] = dsw
            for n in range(near):
                dsm[n * 256:(n + 1) * 256, gl] = dsp * mrow[n]

    halves = [pl.ds(h * LANES, LANES) for h in range(KVH)]

    def query_grad(h):
        hc = slice(h * HEAD, (h + 1) * HEAD)
        keys = jnp.concatenate(kp[h] + [wk[:, hc]], axis=0)
        dqt = dot(keys, dsm[...], 0, 0) * SCALE
        gqt = dqt.astype(BF)
        for g in range(GROUP):
            head = h * GROUP + g
            gqall[0, 0, head * HEAD:(head + 1) * HEAD, :] = gqt[:, g * HEAD:(g + 1) * HEAD]
        mine = gqall.at[0, 0, halves[h]]
        copies = {d: send(mine, gqall.at[d, 0, halves[h]], device(dx=d)) for d in (1, 3)}
        copies[0] = send(mine, gqall.at[0, 1, halves[h]], device(flip=True))
        for g in range(GROUP):
            head = h * GROUP + g
            gq_ref[:, head * HEAD:(head + 1) * HEAD] = dqt[:, g * HEAD:(g + 1) * HEAD].T.astype(BF)
        return copies

    def pass_on(h, copies):
        out = []
        for d, lo in ((1, h * LANES), (3, h * LANES + LANES // 2)):
            copies[d].wait_recv()
            rows = pl.ds(lo, LANES // 2)
            out.append(send(gqall.at[d, 0, rows], gqall.at[2, 0, rows], device(dx=d)))
        flips = {
            d: send(gqall.at[d, 0, halves[h]], gqall.at[d, 1, halves[h]], device(flip=True))
            for d in (1, 3)
        }
        return out, flips

    def key_grad(h):
        hc = slice(h * HEAD, (h + 1) * HEAD)
        dv = dot(pbuf[0:256, :], gm[h, :, 0:near * HEAD], 1, 0)
        dk = dot(dsbuf[...], qm[h, :, 0:near * HEAD], 1, 0) * SCALE
        for n in range(near):
            acc[n, h, :, 0:HEAD] = dk[:, n * HEAD:(n + 1) * HEAD]
            acc[n, h, :, HEAD:] = dv[:, n * HEAD:(n + 1) * HEAD]
        for xs in range(NX):
            for n in range(wide):
                csend[h, xs, n] = term(h, n, xs * 2 + oc).astype(BF)
        copy = send(csend.at[h], crecv.at[h], device(flip=True))
        accw[0, :, hc] = dot(dsm[near * 256:, :], qm[h, :, near * HEAD:], 1, 0) * SCALE
        accw[1, :, hc] = dot(pbuf[256:512, :], gm[h, :, near * HEAD:], 1, 0)
        return copy

    def term(h, n, row):
        rows = pl.ds(pl.multiple_of(row * PROWS, PROWS), PROWS)
        return acc[pl.ds(held[n], 1), h, rows, :][0]

    def over_x(h, copy):
        copy.wait_recv()
        for n in range(wide):
            for xs in range(NX):
                total = term(h, n, xs * 2 + c) + crecv[h, xs, n].astype(F32)
                xown[h, xs, n] = total
                xsend[h, xs, n] = total.astype(BF)
        return [
            send(xsend.at[h, lax.rem(x + d, NX)], xrecv.at[h, d - 1], device(dx=d)) for d in (1, 3, 2)
        ]

    def pick(h, target):
        index = jnp.int32(wide)
        for n in range(wide):
            hit = (slot_of[n] == target) & (pg + n < PROMPTS)
            index = jnp.where(hit, n, index)
        return gsum[h, pl.ds(index, 1)][0]

    def over_z(h, copies):
        arrive(copies)
        for n in range(wide):
            total = xown[h, pl.ds(x, 1), n][0]
            for e in range(3):
                total = total + xrecv[h, e, n].astype(F32)
            gsum[h, n] = total
        gsum[h, wide] = jnp.zeros(gsum.shape[2:], F32)
        out = []
        for dz in far:
            zsend[h, dz - 1] = pick(h, lax.rem(z + dz, NZ)).astype(BF)
            out.append(send(zsend.at[h, dz - 1], zrecv.at[h, dz - 1], device(dz=dz)))
        return out

    def yrows(e):
        return pl.ds(pl.multiple_of(lax.rem(y + e, NY) * BLK, 16), BLK)

    def chunk(d):
        both = jnp.concatenate([gqall[d, 0], gqall[d, 1]], axis=1)
        out = dot(wall[...].reshape(NZ * WROWS, QCOLS), both, 1, 0)
        for e in range(2):
            part[d, e] = out[:, e * TOK:(e + 1) * TOK]
            ysend[d, e] = out[:, e * TOK:(e + 1) * TOK].astype(BF)
        up, down = device(dy=1), device(dy=3)
        return [
            send(ysend.at[d, 0, yrows(2)], yrecv.at[d, 0], up),
            send(ysend.at[d, 1, yrows(2)], yrecv.at[d, 1], down),
            send(ysend.at[d, 1, yrows(1)], yrecv.at[d, 2], up),
            send(ysend.at[d, 0, yrows(3)], yrecv.at[d, 3], down),
        ]

    def relay(d, copies):
        copies[0].wait_recv()
        ycomb[d, 0] = (part[d, 0, yrows(1), :] + yrecv[d, 0].astype(F32)).astype(BF)
        copies.append(send(ycomb.at[d, 0], yrecv.at[d, 4], device(dy=1)))
        copies[1].wait_recv()
        ycomb[d, 1] = (part[d, 1, yrows(3), :] + yrecv[d, 1].astype(F32)).astype(BF)
        copies.append(send(ycomb.at[d, 1], yrecv.at[d, 5], device(dy=3)))

    def finish(d, copies):
        arrive(copies[2:])
        own = yrows(0)
        owner_x = lax.rem(x + NX - d, NX)
        out = []
        for e, (a, b) in enumerate(((4, 3), (2, 5))):
            total = part[d, e, own, :] + yrecv[d, a].astype(F32) + yrecv[d, b].astype(F32)
            if d == 0 and e == 0:
                ogi[pl.ds(gidx, 1)] = total.astype(BF)[None]
            else:
                osend[d, e] = total.astype(BF)
                target = (z * 8 + owner_x * 2 + (oc if e else c), y)
                out.append(send(osend.at[d, e], ogi.at[gidx], target))
        return out

    softmax(0)
    gin0 = query_grad(0)
    advance(1, 1)
    c_in0 = key_grad(0)
    softmax(1)
    gin1 = query_grad(1)
    advance(2, 0)
    c_in1 = key_grad(1)
    wsend[...] = accw[:, 0:TOK, :].astype(BF)
    back = send(wsend, wrecv, prv)
    advance(2, 1)
    gx0, gf0 = pass_on(0, gin0)
    store(gq_ref, gq_hbm)
    advance(3, 0)
    advance(3, 1)
    gx1, gf1 = pass_on(1, gin1)
    arrive([gin0[0], gin1[0]])
    arrive(ring_in[3, 0] + ring_in[3, 1])
    x_in0 = over_x(0, c_in0)
    x_in1 = over_x(1, c_in1)
    y0 = chunk(0)
    arrive([gf0[1], gf1[1]])
    y1 = chunk(1)
    arrive([gf0[3], gf1[3]])
    y3 = chunk(3)
    arrive(gx0 + gx1)
    opposite = send(gqall.at[2, 0], gqall.at[2, 1], device(flip=True))
    relay(0, y0)
    arrive([opposite])
    y2 = chunk(2)
    relay(1, y1)
    relay(3, y3)
    z_in0 = over_z(0, x_in0)
    relay(2, y2)
    z_in1 = over_z(1, x_in1)
    o_in = finish(0, y0)
    o_in += finish(1, y1)
    o_in += finish(3, y3)

    back.wait_recv()
    gk_ref[...] = (accw[0, TOK:, :] + wrecv[0].astype(F32)).astype(BF)
    gv_ref[...] = (accw[1, TOK:, :] + wrecv[1].astype(F32)).astype(BF)
    store(gk_ref, gk_hbm)
    store(gv_ref, gv_hbm)
    o_in += finish(2, y2)

    arrive(z_in0 + z_in1)
    for h in range(KVH):
        total = pick(h, z)
        for e in range(NZ - 1):
            total = total + zrecv[h, e].astype(F32)
        gpk_ref[:, h * HEAD:(h + 1) * HEAD] = total[:, 0:HEAD].astype(BF)
        gpv_ref[:, h * HEAD:(h + 1) * HEAD] = total[:, HEAD:].astype(BF)
    store(gpk_ref, gpk_hbm)
    store(gpv_ref, gpv_hbm)

    arrive(o_in)
    blocks = []
    for zz in range(2):
        for j in range(8):
            blocks.append(ogi[j, zz * WROWS:(zz + 1) * WROWS, :])
    git = jnp.concatenate(blocks, axis=0)
    for i in range(QCOLS // HEAD):
        gi_ref[:, i * HEAD:(i + 1) * HEAD] = git[i * HEAD:(i + 1) * HEAD, :].astype(F32).T.astype(BF)
    store(gi_ref, gi_hbm)
    for copy in sent:
        copy.wait_send()
    for copy in stores:
        copy.wait()
    assert count[0] <= nsem


def settle_kernel(count, *refs):
    held = refs[2 * count:3 * count]
    sem = refs[-1]
    inward = [pltpu.make_async_copy(refs[i], held[i], sem.at[0, i]) for i in range(count)]
    for copy in inward:
        copy.start()
    outward = [
        pltpu.make_async_copy(held[i], refs[count + i], sem.at[1, i]) for i in range(count)
    ]
    for i in range(count):
        inward[i].wait()
        outward[i].start()
    for copy in outward:
        copy.wait()


def settle(arrays):
    hb = pl.BlockSpec(memory_space=pl.ANY)
    count = len(arrays)
    return pl.pallas_call(
        functools.partial(settle_kernel, count),
        out_shape=tuple(jax.ShapeDtypeStruct(a.shape, a.dtype) for a in arrays),
        in_specs=[hb] * count,
        out_specs=(hb,) * count,
        scratch_shapes=[pltpu.VMEM(a.shape, a.dtype) for a in arrays]
        + [pltpu.SemaphoreType.DMA((2, count))],
        compiler_params=pltpu.CompilerParams(vmem_limit_bytes=64 * 2**20),
    )(*arrays)


def fused(near, wide, cid, queries, keys, values, output_gradient, pk, pv, weight, lengths, owner):
    nsem = 120
    vm = pl.BlockSpec(memory_space=pltpu.VMEM)
    sm = pl.BlockSpec(memory_space=pltpu.SMEM)
    hb = pl.BlockSpec(memory_space=pl.ANY)
    shape = jax.ShapeDtypeStruct
    results = [(TOK, QCOLS), (TOK, 256), (TOK, 256), (PROWS, 256), (PROWS, 256), (TOK, QCOLS)]
    scratch = [pltpu.VMEM((TOK, QCOLS), BF), pltpu.VMEM((TOK, QCOLS), BF)]
    scratch += [pltpu.VMEM(r, BF) for r in results]
    scratch += [
        pltpu.VMEM((NZ, PROWS, 256), BF),
        pltpu.VMEM((NZ, PROWS, 256), BF),
        pltpu.VMEM((8, wide, PROWS, 256), BF),
        pltpu.VMEM((8, wide, PROWS, 256), BF),
        pltpu.VMEM((2 * TOK, 256), BF),
        pltpu.VMEM((2 * TOK, 256), BF),
        pltpu.VMEM((NZ, WROWS, QCOLS), BF),
        pltpu.VMEM((NX, 2, QCOLS, TOK), BF),
        pltpu.VMEM((KVH, LANES, (near + 1) * HEAD), BF),
        pltpu.VMEM((KVH, LANES, (near + 1) * HEAD), BF),
        pltpu.VMEM((KVH, 512, LANES), F32),
        pltpu.VMEM((KVH, 512, LANES), F32),
        pltpu.VMEM((512, LANES), BF),
        pltpu.VMEM((256, LANES), BF),
        pltpu.VMEM(((near + 1) * 256, LANES), BF),
        pltpu.VMEM((near + 1, KVH, 256, 256), F32),
        pltpu.VMEM((2, 2 * TOK, 256), F32),
        pltpu.VMEM((2, TOK, 256), BF),
        pltpu.VMEM((2, TOK, 256), BF),
        pltpu.VMEM((KVH, NX, wide, PROWS, 256), BF),
        pltpu.VMEM((KVH, NX, wide, PROWS, 256), BF),
        pltpu.VMEM((KVH, NX, wide, PROWS, 256), F32),
        pltpu.VMEM((KVH, NX, wide, PROWS, 256), BF),
        pltpu.VMEM((KVH, NX - 1, wide, PROWS, 256), BF),
        pltpu.VMEM((KVH, wide + 1, PROWS, 256), F32),
        pltpu.VMEM((KVH, NZ - 1, PROWS, 256), BF),
        pltpu.VMEM((KVH, NZ - 1, PROWS, 256), BF),
        pltpu.VMEM((NX, 2, NZ * WROWS, TOK), F32),
        pltpu.VMEM((NX, 2, NZ * WROWS, TOK), BF),
        pltpu.VMEM((NX, 2, BLK, TOK), BF),
        pltpu.VMEM((NX, 6, BLK, TOK), BF),
        pltpu.VMEM((NX, 2, BLK, TOK), BF),
        pltpu.VMEM((8, BLK, TOK), BF),
        pltpu.SemaphoreType.DMA((nsem,)),
        pltpu.SemaphoreType.DMA((nsem,)),
        pltpu.SemaphoreType.DMA((13,)),
    ]
    results = pl.pallas_call(
        functools.partial(kernel, near, wide, nsem),
        out_shape=tuple(shape(r, BF) for r in results),
        in_specs=[hb] * 7 + [vm] + [sm] * 2,
        out_specs=(hb,) * 6,
        scratch_shapes=scratch,
        compiler_params=pltpu.CompilerParams(
            collective_id=cid, has_side_effects=True, vmem_limit_bytes=64 * 2**20
        ),
    )(
        queries, keys, values, output_gradient, pk, pv, weight,
        lengths.reshape(1, RESPONSES), lengths, owner,
    )
    return settle(results)


def few_prompts(lengths):
    tokens = jnp.sum(lengths.reshape(PROMPTS, RESP_PER), axis=1)
    return jnp.min(tokens) >= 4 * TOK


def shards(*args):
    return lax.cond(
        few_prompts(args[7]),
        functools.partial(fused, 2, 3, 0),
        functools.partial(fused, 6, 6, 1),
        *args,
    )


def solution(mesh):
    split = P("dp", "tensor")
    return jax.shard_map(
        shards,
        mesh=mesh,
        in_specs=(split,) * 7 + (P(), P()),
        out_specs=(split,) * 6,
        check_vma=False,
    )
```
